32 devices in a mesh: groups: 2 (over y), seq: 4 (over z), qblk: 2 (over x), sub: 2 (over core).
Axes of the slice: x: 2, y: 2, z: 4, core: 2. Of those that a mesh axis runs over, the one named last changes fastest.
Arguments:
- queries: bfloat16 [8, 512, 32, 128], P(('groups', 'qblk', 'sub'), 'seq'), parts along dimension 0, may hold values from -9 to 9
- keys: bfloat16 [8, 512, 32, 128], P(('groups', 'qblk', 'sub'), 'seq'), parts along dimension 0, may hold values from -9 to 9
- values: bfloat16 [8, 512, 32, 128], P(('groups', 'qblk', 'sub'), 'seq'), parts along dimension 0, may hold values from -6 to 6
- vert_idx: int32 [64, 2], P('groups'), parts along dimension 0, may hold values from 0 to 15, as said below
- vert_cnt: int32 [64], P('groups'), parts along dimension 0, may hold values from 1 to 2, as said below
- slash_off: int32 [64, 2], P('groups'), parts along dimension 0, may hold values from 1 to 4, as said below
- slash_cnt: int32 [64], P('groups'), parts along dimension 0, may hold values from 1 to 2, as said below
Outputs:
- attended: bfloat16 [8, 512, 32, 128], P(('groups', 'qblk', 'sub'), 'seq'), parts along dimension 0
The draws below stay inside these ranges and needn't reach their ends.
There are 2 independent parts, one for each index of `groups`. The reference program is written for one: setup_inputs(seed, part) draws one part's arguments, and reference() takes and returns one part's arrays. A program takes and returns all parts, laid end to end along the dimension named above; each array names one. Nothing has to cross between parts.
Inputs may be any that keep to these rules, and one draw needn't show every extreme that they name: `vert_idx`: per head the first vert_cnt entries are distinct block indices; some head lists block 0 and block 15. `vert_cnt`: some head uses all 2 entries; most heads use one or two. `slash_off`: per head the first slash_cnt entries are distinct; some head lists offset 4. `slash_cnt`: some head uses all 2 entries.
All inputs are finite; a program needn't handle non-finite values.
Results may differ from the reference program's by a relative error of at most 0.0034.
Values may be sent and summed in bfloat16 or wider, within the bound.
No kernel may reach another device: no remote copies, remote signals or barrier semaphores. Data moves between devices by JAX's collectives and lax.ppermute only.
A program may use at most 64 MiB of HBM per device.

```python
import jax
import jax.numpy as jnp
from jax import lax

H = 32
DH = 128
BLK = 128
NA = 4
SPAN = 512
PB = 4
NB = 16
MAXV = 2
MAXS = 2


def draw_queries(key, part):
    key = jax.random.fold_in(key, 3)
    return jnp.clip(1.5 * jax.random.normal(key, (NA, SPAN, H, DH), jnp.float32), -9.0, 9.0).astype(jnp.bfloat16)


def draw_keys(key, part):
    key = jax.random.fold_in(key, 5)
    return jnp.clip(1.5 * jax.random.normal(key, (NA, SPAN, H, DH), jnp.float32), -9.0, 9.0).astype(jnp.bfloat16)


def vertical_plan(key):
    key = jax.random.fold_in(key, 101)
    key_a, key_b, key_c, key_d, key_e = jax.random.split(key, 5)
    head_ids = jnp.arange(H, dtype=jnp.int32)
    heavy = jax.random.randint(key_a, (H,), 0, 4) == 0
    counts = jnp.where(heavy, jax.random.randint(key_b, (H,), max(MAXV // 2, 1), MAXV + 1), jnp.minimum(jax.random.randint(key_c, (H,), 1, 3), MAXV))
    forced = jax.random.randint(key_d, (), 0, H)
    counts = jnp.where(head_ids == forced, MAXV, counts)
    block_ids = jnp.arange(NB, dtype=jnp.int32)
    noise = jax.random.randint(key_e, (H, NB), 0, 65536) * NB + block_ids[None, :]
    boost = (head_ids[:, None] == forced) & ((block_ids == 0) | (block_ids == NB - 1))[None, :]
    noise = jnp.where(boost, 65536 * NB + block_ids[None, :], noise)
    picked = lax.top_k(noise, MAXV)[1]
    return (picked.astype(jnp.int32), counts.astype(jnp.int32))


def slash_plan(key):
    key = jax.random.fold_in(key, 202)
    key_a, key_b, key_c, key_d, key_e = jax.random.split(key, 5)
    head_ids = jnp.arange(H, dtype=jnp.int32)
    heavy = jax.random.randint(key_a, (H,), 0, 4) == 0
    light = jax.random.randint(key_c, (H,), 1, 3)
    counts = jnp.where(heavy, jax.random.randint(key_b, (H,), max(MAXS // 2, 1), MAXS + 1), light)
    forced = jax.random.randint(key_d, (), 0, H)
    counts = jnp.where(head_ids == forced, MAXS, counts)
    offset_ids = jnp.arange(PB, dtype=jnp.int32)
    noise = jax.random.randint(key_e, (H, PB), 0, 65536) * PB + offset_ids[None, :]
    boost = (head_ids[:, None] == forced) & (offset_ids == PB - 1)[None, :]
    noise = jnp.where(boost, 65536 * PB + offset_ids[None, :], noise)
    picked = lax.top_k(noise, MAXS)[1] + 1
    return (picked.astype(jnp.int32), counts.astype(jnp.int32))


def draw_vert_idx(key, part):
    return vertical_plan(key)[0]


def draw_vert_cnt(key, part):
    return vertical_plan(key)[1]


def draw_slash_off(key, part):
    return slash_plan(key)[0]


def draw_slash_cnt(key, part):
    return slash_plan(key)[1]


def block_levels(own_key, dims, pieces, least, high):
    level, own = 1.0, jax.random.fold_in(own_key, 6)
    for axis_at, shards_of in pieces:
        draws = jnp.exp(jax.random.uniform(jax.random.fold_in(own, axis_at), (shards_of,), jnp.float32, least / len(pieces), high / len(pieces)))
        level = level * jnp.repeat(draws, dims[axis_at] // shards_of).reshape([-1 if axis == axis_at else 1 for axis in range(len(dims))])
    return level


def scatter_about(key, dims, deviation, reach, cuts=(), kind=jnp.bfloat16):
    array = deviation * jax.random.normal(key, dims, jnp.float32)
    if cuts:
        array = array * block_levels(key, dims, cuts, -0.22, 0.18)
    return jnp.clip(array, -reach, reach).astype(kind)


def setup_inputs(seed: int = 0, part: int = 0) -> dict:
    key_list = jax.random.split(jax.random.key(seed), 8)
    own_keys = jax.random.split(jax.random.fold_in(key_list[7], part), 8)
    return {
        "queries": draw_queries(jax.random.fold_in(jax.random.fold_in(key_list[7], part), 71), part),
        "keys": draw_keys(jax.random.fold_in(jax.random.fold_in(key_list[7], part), 71), part),
        "values": scatter_about(own_keys[2], (NA, SPAN, H, DH), 1.0, 6.0, ((0, 4), (1, 4))),
        "vert_idx": draw_vert_idx(jax.random.fold_in(jax.random.fold_in(key_list[7], part), 71), part),
        "vert_cnt": draw_vert_cnt(jax.random.fold_in(jax.random.fold_in(key_list[7], part), 71), part),
        "slash_off": draw_slash_off(jax.random.fold_in(jax.random.fold_in(key_list[7], part), 71), part),
        "slash_cnt": draw_slash_cnt(jax.random.fold_in(jax.random.fold_in(key_list[7], part), 71), part),
    }


def head_attention(q_head, k_head, v_head, v_list, v_count, s_list, s_count):
    block_ids = jnp.arange(NB, dtype=jnp.int32)
    s_live = jnp.arange(MAXS, dtype=jnp.int32) < s_count
    slash_table = jnp.any((s_list[None, :] == jnp.arange(PB + 1, dtype=jnp.int32)[:, None]) & s_live[None, :], axis=1)
    s_cols = block_ids[:, None] - s_list[None, :]
    s_valid = s_live[None, :] & (s_cols >= 0)
    distance = block_ids[:, None] - v_list[None, :]
    in_slash = (distance <= PB) & slash_table[jnp.clip(distance, 0, PB).astype(jnp.int32)]
    v_valid = (jnp.arange(MAXV, dtype=jnp.int32) < v_count)[None, :] & (distance > 0) & jnp.logical_not(in_slash)
    v_cols = jnp.broadcast_to(v_list[None, :], (NB, MAXV))
    columns = jnp.concatenate([block_ids[:, None], s_cols, v_cols], axis=1)
    columns = jnp.clip(columns, 0, NB - 1).astype(jnp.int32)
    valid = jnp.concatenate([jnp.ones((NB, 1), dtype=bool), s_valid, v_valid], axis=1)
    k_sel = k_head[columns].astype(jnp.float32)
    v_sel = v_head[columns].astype(jnp.float32)
    scores = jnp.einsum("nid,ncjd->nicj", q_head.astype(jnp.float32), k_sel) * (DH ** -0.5)
    causal = jnp.arange(BLK)[:, None] >= jnp.arange(BLK)[None, :]
    width_cols = valid.shape[1]
    later_col = jnp.arange(width_cols) > 0
    key_mask = valid[:, None, :, None] & (later_col[None, None, :, None] | causal[None, :, None, :])
    scores = jnp.where(key_mask, scores, -jnp.inf)
    row_max = jnp.max(scores, axis=(2, 3))
    weights = jnp.exp(scores - row_max[:, :, None, None])
    run_sum = jnp.sum(weights, axis=(2, 3))
    rounded = lax.optimization_barrier(weights.astype(jnp.bfloat16)).astype(jnp.float32)
    output = jnp.einsum("nicj,ncjd->nid", rounded, v_sel) / run_sum[:, :, None]
    return output.astype(jnp.bfloat16)


def arrange(tensor):
    return tensor.reshape(NB, BLK, H, DH).transpose(2, 0, 1, 3)


def one_head(item):
    return head_attention(*item)


def reference(queries, keys, values, vert_idx, vert_cnt, slash_off, slash_cnt):
    outputs = lax.map(one_head, (arrange(queries), arrange(keys), arrange(values), vert_idx, vert_cnt, slash_off, slash_cnt))
    return outputs.transpose(1, 2, 0, 3).reshape(NA, SPAN, H, DH)
```

```python
import functools

import jax
import jax.numpy as jnp
from jax import lax
from jax.experimental import pallas as pl
from jax.experimental.pallas import tpu as pltpu
from jax.sharding import PartitionSpec as P

BLK = 128


NEG_START = -1e30


def from_behind(value, axis, steps):
    count = lax.axis_size(axis)
    initial, last = (max(0, -steps), min(count, count - steps))
    return lax.ppermute(value, axis, [(source, source + steps) for source in range(initial, last)])


def pick_rows(table, chosen):
    heads = table.shape[0]
    onehot = chosen[:, None] == jnp.arange(heads, dtype=jnp.int32)[None, :]
    if table.ndim == 1:
        return jnp.sum(jnp.where(onehot, table[None, :], 0), axis=1)
    return jnp.sum(jnp.where(onehot[:, :, None], table[None, :, :], 0), axis=1)


def absorb(carry_state, scores, key_mask, tile_vals, einsum_form):
    run_max, run_sum, run_acc = carry_state
    scores = jnp.where(key_mask, scores, -jnp.inf)
    new_max = jnp.maximum(run_max, jnp.max(scores, axis=-1))
    factor = jnp.exp(run_max - new_max)
    weights = jnp.exp(scores - new_max[..., None])
    run_sum = run_sum * factor + jnp.sum(weights, axis=-1)
    run_acc = run_acc * factor[..., None] + jnp.einsum(
        einsum_form, weights.astype(jnp.bfloat16), tile_vals, preferred_element_type=jnp.float32
    )
    return (new_max, run_sum, run_acc)


def attend_head(
    q_head,
    k_head,
    v_head,
    key_prev,
    val_prev,
    sink_k,
    sink_v,
    v_list,
    v_count,
    s_list,
    s_count,
    slash_table,
    first_block,
):
    span_rows, head_width = q_head.shape
    span_blocks = span_rows // BLK
    scaling = head_width ** (-0.5)
    q_blocks = q_head.reshape(span_blocks, BLK, head_width)
    block_ids = first_block + jnp.arange(span_blocks, dtype=jnp.int32)
    carry_state = (
        jnp.full((span_blocks, BLK), NEG_START, jnp.float32),
        jnp.zeros((span_blocks, BLK), jnp.float32),
        jnp.zeros((span_blocks, BLK, head_width), jnp.float32),
    )
    k_blocks = k_head.reshape(span_blocks, BLK, head_width)
    v_blocks = v_head.reshape(span_blocks, BLK, head_width)
    scores = (
        jnp.einsum("pid,pjd->pij", q_blocks, k_blocks, preferred_element_type=jnp.float32) * scaling
    )
    causal = jnp.arange(BLK)[:, None] >= jnp.arange(BLK)[None, :]
    carry_state = absorb(carry_state, scores, causal[None], v_blocks, "pij,pjd->pid")
    ext_k = jnp.concatenate([key_prev, k_head], axis=0)
    ext_v = jnp.concatenate([val_prev, v_head], axis=0)

    def slash_step(turn_index, carry_state):
        offset = s_list[turn_index]
        start_row = span_rows - offset * BLK
        k_tile = lax.dynamic_slice_in_dim(ext_k, start_row, span_rows, 0).reshape(
            span_blocks, BLK, head_width
        )
        v_tile = lax.dynamic_slice_in_dim(ext_v, start_row, span_rows, 0).reshape(
            span_blocks, BLK, head_width
        )
        tile_scores = (
            jnp.einsum("pid,pjd->pij", q_blocks, k_tile, preferred_element_type=jnp.float32)
            * scaling
        )
        key_mask = (block_ids - offset >= 0)[:, None, None]
        return absorb(carry_state, tile_scores, key_mask, v_tile, "pij,pjd->pid")

    carry_state = lax.fori_loop(0, s_count, slash_step, carry_state)

    def vertical_step(turn_index, carry_state):
        column = v_list[turn_index]
        k_tile = sink_k[turn_index]
        v_tile = sink_v[turn_index]
        tile_scores = (
            jnp.einsum("pid,jd->pij", q_blocks, k_tile, preferred_element_type=jnp.float32)
            * scaling
        )
        distance = block_ids - column
        in_slash = (distance <= span_blocks) & slash_table[jnp.clip(distance, 0, span_blocks)]
        key_mask = ((distance > 0) & jnp.logical_not(in_slash))[:, None, None]
        return absorb(carry_state, tile_scores, key_mask, v_tile, "pij,jd->pid")

    carry_state = lax.fori_loop(0, v_count, vertical_step, carry_state)
    run_max, run_sum, run_acc = carry_state
    return (run_acc / run_sum[..., None]).astype(jnp.bfloat16).reshape(span_rows, head_width)


def spans_body(queries, keys, values, vert_idx, vert_cnt, slash_off, slash_cnt):
    n_seq = lax.axis_size("seq")
    heads = queries.shape[2]
    per_dev = heads // n_seq
    head_order = jnp.arange(heads, dtype=jnp.int32)
    q_all, k_all, v_all = (
        lax.all_to_all(queries, "seq", split_axis=2, concat_axis=1, tiled=True),
        lax.all_to_all(keys, "seq", split_axis=2, concat_axis=1, tiled=True),
        lax.all_to_all(values, "seq", split_axis=2, concat_axis=1, tiled=True),
    )
    key_prev, val_prev = from_behind((k_all, v_all), ("qblk", "sub"), 1)
    span_rows = q_all.shape[1]
    head_width = q_all.shape[3]
    span_blocks = span_rows // BLK
    first_block = lax.axis_index(("qblk", "sub")) * span_blocks
    my_heads = lax.dynamic_slice_in_dim(head_order, lax.axis_index("seq") * per_dev, per_dev)
    v_lists = pick_rows(vert_idx, my_heads)
    v_counts = pick_rows(vert_cnt, my_heads)
    s_lists = pick_rows(slash_off, my_heads)
    s_counts = pick_rows(slash_cnt, my_heads)
    local_ids = v_lists - first_block
    owned = (local_ids >= 0) & (local_ids < span_blocks)
    clipped = jnp.clip(local_ids, 0, span_blocks - 1)
    slot_ids = jnp.arange(per_dev, dtype=jnp.int32)[:, None]
    k_grid = k_all[0].reshape(span_blocks, BLK, per_dev, head_width)
    v_grid = v_all[0].reshape(span_blocks, BLK, per_dev, head_width)
    zero_half = jnp.zeros((), jnp.bfloat16)
    picked_k = jnp.where(owned[:, :, None, None], k_grid[clipped, :, slot_ids, :], zero_half)
    picked_v = jnp.where(owned[:, :, None, None], v_grid[clipped, :, slot_ids, :], zero_half)
    sink_k, sink_v = (
        lax.psum(picked_k, ("qblk", "sub")).astype(jnp.float32),
        lax.psum(picked_v, ("qblk", "sub")).astype(jnp.float32),
    )
    sink_k = sink_k.astype(jnp.bfloat16)
    sink_v = sink_v.astype(jnp.bfloat16)
    s_width = slash_off.shape[1]
    s_live = jnp.arange(s_width, dtype=jnp.int32)[None, :] < s_counts[:, None]
    offset_ids = jnp.arange(span_blocks + 1, dtype=jnp.int32)
    slash_tables = jnp.any(
        (s_lists[:, :, None] == offset_ids[None, None, :]) & s_live[:, :, None], axis=1
    )
    results = []
    for slot in range(per_dev):
        results.append(
            attend_head(
                q_all[0, :, slot, :],
                k_all[0, :, slot, :],
                v_all[0, :, slot, :],
                key_prev[0, :, slot, :],
                val_prev[0, :, slot, :],
                sink_k[slot],
                sink_v[slot],
                v_lists[slot],
                v_counts[slot],
                s_lists[slot],
                s_counts[slot],
                slash_tables[slot],
                first_block,
            )
        )
    stacked = jnp.stack(results, axis=1)[None]
    restored = lax.all_to_all(stacked, "seq", split_axis=1, concat_axis=2, tiled=True)
    return restored


PROMPT = ("qblk", "sub", "seq")


def pair_scores(q, k_cols, scaling):
    return lax.dot_general(
        q, k_cols, (((1,), (1,)), ((), ())), preferred_element_type=jnp.float32
    ) * scaling


def attend_kernel(vert_idx, vert_cnt, slash_off, slash_cnt, qkv, out, *, scaling):
    blocks, _, heads = qkv.shape[:3]
    n_vert, n_slash = vert_idx.shape[1], slash_off.shape[1]
    row = lax.broadcasted_iota(jnp.int32, (BLK, BLK), 0)
    col = lax.broadcasted_iota(jnp.int32, (BLK, BLK), 1)
    causal = row >= col

    def unit(head, block):
        cols, live = [block], []
        for turn in range(n_slash):
            offset = slash_off[head, turn]
            live.append((turn < slash_cnt[head]) & (block >= offset))
            cols.append(jnp.maximum(block - offset, 0))
        for turn in range(n_vert):
            column = vert_idx[head, turn]
            distance = block - column
            ok = (turn < vert_cnt[head]) & (distance > 0)
            for other in range(n_slash):
                hit = (other < slash_cnt[head]) & (slash_off[head, other] == distance)
                ok = ok & jnp.logical_not(hit)
            live.append(ok)
            cols.append(column)
        q = qkv[block, 0, head]
        parts = [jnp.where(causal, pair_scores(q, qkv[block, 1, head], scaling), -jnp.inf)]
        for column, ok in zip(cols[1:], live):
            bias = jnp.where(ok, 0.0, -jnp.inf).astype(jnp.float32)
            parts.append(pair_scores(q, qkv[column, 1, head], scaling) + bias)
        scores = jnp.concatenate(parts, axis=1)
        top = jnp.max(scores, axis=1, keepdims=True)
        weights = jnp.exp(scores - top)
        total = jnp.sum(weights, axis=1, keepdims=True)
        vals = jnp.concatenate([qkv[column, 2, head] for column in cols], axis=0)
        acc = jnp.dot(weights.astype(jnp.bfloat16), vals, preferred_element_type=jnp.float32)
        out[block, head] = (acc / total).astype(jnp.bfloat16)

    for head in range(heads):
        @pl.loop(0, blocks // 4)
        def _(step):
            for inner in range(4):
                unit(head, step * 4 + inner)


def prompt_body(queries, keys, values, vert_idx, vert_cnt, slash_off, slash_cnt):
    count = lax.axis_size(PROMPT)
    heads, width = queries.shape[2:]
    per_dev = heads // count
    stacked = jnp.concatenate([queries, keys, values], axis=0)
    stacked = stacked.reshape(3, BLK, count, per_dev, width).transpose(2, 0, 3, 1, 4)
    qkv = lax.all_to_all(stacked, PROMPT, split_axis=0, concat_axis=0, tiled=True)
    first = lax.axis_index(PROMPT) * per_dev
    tables = [
        lax.dynamic_slice_in_dim(table, first, per_dev, 0)
        for table in (vert_idx, vert_cnt, slash_off, slash_cnt)
    ]
    smem = pl.BlockSpec(memory_space=pltpu.SMEM)
    vmem = pl.BlockSpec(memory_space=pltpu.VMEM)
    attended = pl.pallas_call(
        functools.partial(attend_kernel, scaling=width ** (-0.5)),
        out_shape=jax.ShapeDtypeStruct((count, per_dev, BLK, width), jnp.bfloat16),
        in_specs=[smem] * 4 + [vmem],
        out_specs=vmem,
        compiler_params=pltpu.CompilerParams(vmem_limit_bytes=24 * 2**20),
        name="attend",
    )(*tables, qkv)
    back = lax.all_to_all(attended, PROMPT, split_axis=0, concat_axis=0, tiled=True)
    return back.reshape(heads, BLK, width).transpose(1, 0, 2)[None]


def body(queries, keys, values, *tables):
    devices = lax.axis_size(PROMPT)
    if queries.shape[2] % devices == 0 and queries.shape[:2] == (1, BLK):
        return prompt_body(queries, keys, values, *tables)
    return spans_body(queries, keys, values, *tables)


def solution(mesh):
    placed = (
        P(("groups", "qblk", "sub"), "seq", None, None),
        P(("groups", "qblk", "sub"), "seq", None, None),
        P(("groups", "qblk", "sub"), "seq", None, None),
        P("groups", None),
        P("groups"),
        P("groups", None),
        P("groups"),
    )
    return jax.shard_map(
        body,
        mesh=mesh,
        in_specs=placed,
        out_specs=P(("groups", "qblk", "sub"), "seq", None, None),
        check_vma=False,
    )
```

```python
import functools

import jax
import jax.numpy as jnp
from jax import lax
from jax.experimental import pallas as pl
from jax.experimental.pallas import tpu as pltpu
from jax.sharding import PartitionSpec as P

BLK = 128


NEG_START = -1e30


def from_behind(value, axis, steps):
    count = lax.axis_size(axis)
    initial, last = (max(0, -steps), min(count, count - steps))
    return lax.ppermute(value, axis, [(source, source + steps) for source in range(initial, last)])


def pick_rows(table, chosen):
    heads = table.shape[0]
    onehot = chosen[:, None] == jnp.arange(heads, dtype=jnp.int32)[None, :]
    if table.ndim == 1:
        return jnp.sum(jnp.where(onehot, table[None, :], 0), axis=1)
    return jnp.sum(jnp.where(onehot[:, :, None], table[None, :, :], 0), axis=1)


def absorb(carry_state, scores, key_mask, tile_vals, einsum_form):
    run_max, run_sum, run_acc = carry_state
    scores = jnp.where(key_mask, scores, -jnp.inf)
    new_max = jnp.maximum(run_max, jnp.max(scores, axis=-1))
    factor = jnp.exp(run_max - new_max)
    weights = jnp.exp(scores - new_max[..., None])
    run_sum = run_sum * factor + jnp.sum(weights, axis=-1)
    run_acc = run_acc * factor[..., None] + jnp.einsum(
        einsum_form, weights.astype(jnp.bfloat16), tile_vals, preferred_element_type=jnp.float32
    )
    return (new_max, run_sum, run_acc)


def attend_head(
    q_head,
    k_head,
    v_head,
    key_prev,
    val_prev,
    sink_k,
    sink_v,
    v_list,
    v_count,
    s_list,
    s_count,
    slash_table,
    first_block,
):
    span_rows, head_width = q_head.shape
    span_blocks = span_rows // BLK
    scaling = head_width ** (-0.5)
    q_blocks = q_head.reshape(span_blocks, BLK, head_width)
    block_ids = first_block + jnp.arange(span_blocks, dtype=jnp.int32)
    carry_state = (
        jnp.full((span_blocks, BLK), NEG_START, jnp.float32),
        jnp.zeros((span_blocks, BLK), jnp.float32),
        jnp.zeros((span_blocks, BLK, head_width), jnp.float32),
    )
    k_blocks = k_head.reshape(span_blocks, BLK, head_width)
    v_blocks = v_head.reshape(span_blocks, BLK, head_width)
    scores = (
        jnp.einsum("pid,pjd->pij", q_blocks, k_blocks, preferred_element_type=jnp.float32) * scaling
    )
    causal = jnp.arange(BLK)[:, None] >= jnp.arange(BLK)[None, :]
    carry_state = absorb(carry_state, scores, causal[None], v_blocks, "pij,pjd->pid")
    ext_k = jnp.concatenate([key_prev, k_head], axis=0)
    ext_v = jnp.concatenate([val_prev, v_head], axis=0)

    def slash_step(turn_index, carry_state):
        offset = s_list[turn_index]
        start_row = span_rows - offset * BLK
        k_tile = lax.dynamic_slice_in_dim(ext_k, start_row, span_rows, 0).reshape(
            span_blocks, BLK, head_width
        )
        v_tile = lax.dynamic_slice_in_dim(ext_v, start_row, span_rows, 0).reshape(
            span_blocks, BLK, head_width
        )
        tile_scores = (
            jnp.einsum("pid,pjd->pij", q_blocks, k_tile, preferred_element_type=jnp.float32)
            * scaling
        )
        key_mask = (block_ids - offset >= 0)[:, None, None]
        return absorb(carry_state, tile_scores, key_mask, v_tile, "pij,pjd->pid")

    carry_state = lax.fori_loop(0, s_count, slash_step, carry_state)

    def vertical_step(turn_index, carry_state):
        column = v_list[turn_index]
        k_tile = sink_k[turn_index]
        v_tile = sink_v[turn_index]
        tile_scores = (
            jnp.einsum("pid,jd->pij", q_blocks, k_tile, preferred_element_type=jnp.float32)
            * scaling
        )
        distance = block_ids - column
        in_slash = (distance <= span_blocks) & slash_table[jnp.clip(distance, 0, span_blocks)]
        key_mask = ((distance > 0) & jnp.logical_not(in_slash))[:, None, None]
        return absorb(carry_state, tile_scores, key_mask, v_tile, "pij,jd->pid")

    carry_state = lax.fori_loop(0, v_count, vertical_step, carry_state)
    run_max, run_sum, run_acc = carry_state
    return (run_acc / run_sum[..., None]).astype(jnp.bfloat16).reshape(span_rows, head_width)


def spans_body(queries, keys, values, vert_idx, vert_cnt, slash_off, slash_cnt):
    n_seq = lax.axis_size("seq")
    heads = queries.shape[2]
    per_dev = heads // n_seq
    head_order = jnp.arange(heads, dtype=jnp.int32)
    q_all, k_all, v_all = (
        lax.all_to_all(queries, "seq", split_axis=2, concat_axis=1, tiled=True),
        lax.all_to_all(keys, "seq", split_axis=2, concat_axis=1, tiled=True),
        lax.all_to_all(values, "seq", split_axis=2, concat_axis=1, tiled=True),
    )
    key_prev, val_prev = from_behind((k_all, v_all), ("qblk", "sub"), 1)
    span_rows = q_all.shape[1]
    head_width = q_all.shape[3]
    span_blocks = span_rows // BLK
    first_block = lax.axis_index(("qblk", "sub")) * span_blocks
    my_heads = lax.dynamic_slice_in_dim(head_order, lax.axis_index("seq") * per_dev, per_dev)
    v_lists = pick_rows(vert_idx, my_heads)
    v_counts = pick_rows(vert_cnt, my_heads)
    s_lists = pick_rows(slash_off, my_heads)
    s_counts = pick_rows(slash_cnt, my_heads)
    local_ids = v_lists - first_block
    owned = (local_ids >= 0) & (local_ids < span_blocks)
    clipped = jnp.clip(local_ids, 0, span_blocks - 1)
    slot_ids = jnp.arange(per_dev, dtype=jnp.int32)[:, None]
    k_grid = k_all[0].reshape(span_blocks, BLK, per_dev, head_width)
    v_grid = v_all[0].reshape(span_blocks, BLK, per_dev, head_width)
    zero_half = jnp.zeros((), jnp.bfloat16)
    picked_k = jnp.where(owned[:, :, None, None], k_grid[clipped, :, slot_ids, :], zero_half)
    picked_v = jnp.where(owned[:, :, None, None], v_grid[clipped, :, slot_ids, :], zero_half)
    sink_k, sink_v = (
        lax.psum(picked_k, ("qblk", "sub")).astype(jnp.float32),
        lax.psum(picked_v, ("qblk", "sub")).astype(jnp.float32),
    )
    sink_k = sink_k.astype(jnp.bfloat16)
    sink_v = sink_v.astype(jnp.bfloat16)
    s_width = slash_off.shape[1]
    s_live = jnp.arange(s_width, dtype=jnp.int32)[None, :] < s_counts[:, None]
    offset_ids = jnp.arange(span_blocks + 1, dtype=jnp.int32)
    slash_tables = jnp.any(
        (s_lists[:, :, None] == offset_ids[None, None, :]) & s_live[:, :, None], axis=1
    )
    results = []
    for slot in range(per_dev):
        results.append(
            attend_head(
                q_all[0, :, slot, :],
                k_all[0, :, slot, :],
                v_all[0, :, slot, :],
                key_prev[0, :, slot, :],
                val_prev[0, :, slot, :],
                sink_k[slot],
                sink_v[slot],
                v_lists[slot],
                v_counts[slot],
                s_lists[slot],
                s_counts[slot],
                slash_tables[slot],
                first_block,
            )
        )
    stacked = jnp.stack(results, axis=1)[None]
    restored = lax.all_to_all(stacked, "seq", split_axis=1, concat_axis=2, tiled=True)
    return restored


GROUP = ("seq", "qblk")
MIB = 2**20
REGROUP_VMEM = 60 * MIB
ANY = pl.BlockSpec(memory_space=pl.ANY)
HBM = pl.BlockSpec(memory_space=pltpu.HBM)
SMEM = pl.BlockSpec(memory_space=pltpu.SMEM)
VMEM = pl.BlockSpec(memory_space=pltpu.VMEM)


def swap_with(value, axes, mask):
    count = lax.axis_size(axes)
    return lax.ppermute(value, axes, [(source, source ^ mask) for source in range(count)])


def first_head(place, masks, heads, groups):
    half = groups // 2
    return pl.multiple_of(((place[0] ^ masks[0]) // half) * (heads // 2), heads // 2)


def regroup_kernel(place, *refs, tensors, takes, pieces, groups):
    sources, parts = refs[:tensors], refs[tensors : tensors + len(pieces)]
    staged, turned, load_sem, store_sem = refs[tensors + len(pieces) :]
    count, per_group = turned.shape[0], turned.shape[2]
    heads = sources[0].shape[1]
    loads = [
        pltpu.make_async_copy(
            sources[tensor].at[:, pl.ds(first_head(place, masks, heads, groups), heads // 2)],
            staged.at[at],
            load_sem.at[at],
        )
        for at, (masks, tensor) in enumerate(takes)
    ]
    for load in loads:
        load.start()
    stores = []
    for at, load in enumerate(loads):
        load.wait()
        heads_first = jnp.swapaxes(staged[at], 0, 1)
        for group in range(count):
            turned[group, at] = heads_first[group * per_group : (group + 1) * per_group]
        for into, ((mask, begin, length), part) in enumerate(zip(pieces, parts)):
            if begin + length == at + 1:
                part_at = turned.at[(place[0] ^ mask) % count, pl.ds(begin, length)]
                stores.append(pltpu.make_async_copy(part_at, part, store_sem.at[into]))
                stores[-1].start()
    for store in stores:
        store.wait()


def regroup(place, tensors, takes, pieces, groups):
    tokens, heads, width = tensors[0].shape
    part = (heads // groups, tokens, width)
    parts = pl.pallas_call(
        functools.partial(
            regroup_kernel, tensors=len(tensors), takes=takes, pieces=pieces, groups=groups
        ),
        out_shape=[
            jax.ShapeDtypeStruct((length,) + part, jnp.bfloat16) for _, _, length in pieces
        ],
        in_specs=[SMEM] + [HBM] * len(tensors),
        out_specs=[ANY] * len(pieces),
        scratch_shapes=[
            pltpu.VMEM((len(takes), tokens, heads // 2, width), jnp.bfloat16),
            pltpu.VMEM((groups // 2, len(takes)) + part, jnp.bfloat16),
            pltpu.SemaphoreType.DMA((len(takes),)),
            pltpu.SemaphoreType.DMA((len(pieces),)),
        ],
        compiler_params=pltpu.CompilerParams(vmem_limit_bytes=REGROUP_VMEM),
        cost_estimate=pl.CostEstimate(flops=1, bytes_accessed=1, transcendentals=0),
        name="regroup",
    )(place, *tensors)
    return dict(zip(pieces, parts))


def ungroup_half(place, *refs, masks, groups):
    parts = refs[: len(masks)]
    out, staged, turned, load_sem, store_sem = refs[-5:]
    count, per_group, tokens, width = staged.shape
    heads = out.shape[1]
    loads = [
        pltpu.make_async_copy(part, staged.at[(place[0] ^ mask) % count], load_sem.at[at])
        for at, (mask, part) in enumerate(zip(masks, parts))
    ]
    for load in loads:
        load.start()
    for load in loads:
        load.wait()
    heads_first = staged[...].reshape(count * per_group, tokens, width)
    turned[...] = jnp.swapaxes(heads_first, 0, 1)
    first = first_head(place, masks, heads, groups)
    store = pltpu.make_async_copy(turned, out.at[:, pl.ds(first, heads // 2)], store_sem)
    store.start()
    store.wait()


def ungroup(place, parts, masks, groups, begun=None):
    per_group, tokens, width = parts[masks[0]].shape
    shape = (tokens, groups * per_group, width)
    return pl.pallas_call(
        functools.partial(ungroup_half, masks=masks, groups=groups),
        out_shape=jax.ShapeDtypeStruct(shape, jnp.bfloat16),
        in_specs=[SMEM] + [ANY] * len(masks) + ([] if begun is None else [HBM]),
        out_specs=HBM,
        scratch_shapes=[
            pltpu.VMEM((len(masks), per_group, tokens, width), jnp.bfloat16),
            pltpu.VMEM((tokens, len(masks) * per_group, width), jnp.bfloat16),
            pltpu.SemaphoreType.DMA((len(masks),)),
            pltpu.SemaphoreType.DMA,
        ],
        input_output_aliases={} if begun is None else {1 + len(masks): 0},
        compiler_params=pltpu.CompilerParams(vmem_limit_bytes=6 * MIB),
        cost_estimate=pl.CostEstimate(flops=1, bytes_accessed=1, transcendentals=0),
        name="ungroup",
    )(place, *[parts[mask] for mask in masks], *([] if begun is None else [begun]))


def block_of(place, mask, n_seq, n_qblk):
    partner = place[0] ^ mask
    return (2 * (partner % n_qblk) + place[1]) * n_seq + partner // n_qblk


def gather_kernel(place, *refs, groups, n_seq, n_qblk):
    own, out, sem = refs[:groups], refs[groups], refs[groups + 1]
    copies = [
        pltpu.make_async_copy(
            part.at[pl.ds(0, 2)],
            out.at[((place[0] ^ mask) % n_qblk) * n_seq + (place[0] ^ mask) // n_qblk],
            sem.at[mask],
        )
        for mask, part in enumerate(own)
    ]
    for copy in copies:
        copy.start()
    for copy in copies:
        copy.wait()


def gather(place, parts):
    groups = len(parts)
    shape = (groups, 2) + parts[0].shape[1:]
    return pl.pallas_call(
        functools.partial(
            gather_kernel,
            groups=groups,
            n_seq=lax.axis_size("seq"),
            n_qblk=lax.axis_size("qblk"),
        ),
        out_shape=jax.ShapeDtypeStruct(shape, jnp.bfloat16),
        in_specs=[SMEM] + [ANY] * groups,
        out_specs=ANY,
        scratch_shapes=[pltpu.SemaphoreType.DMA((groups,))],
        compiler_params=pltpu.CompilerParams(vmem_limit_bytes=2 * MIB),
        cost_estimate=pl.CostEstimate(flops=1, bytes_accessed=1, transcendentals=0),
        name="gather",
    )(place, *parts)


def join_kernel(place, own, other, out, sem):
    copies = [
        pltpu.make_async_copy(own, out.at[place[1]], sem.at[0]),
        pltpu.make_async_copy(other, out.at[1 - place[1]], sem.at[1]),
    ]
    for copy in copies:
        copy.start()
    for copy in copies:
        copy.wait()


def join(place, own, other):
    return pl.pallas_call(
        join_kernel,
        out_shape=jax.ShapeDtypeStruct((2,) + own.shape, jnp.bfloat16),
        in_specs=[SMEM, ANY, ANY],
        out_specs=ANY,
        scratch_shapes=[pltpu.SemaphoreType.DMA((2,))],
        compiler_params=pltpu.CompilerParams(vmem_limit_bytes=2 * MIB),
        cost_estimate=pl.CostEstimate(flops=1, bytes_accessed=1, transcendentals=0),
        name="join",
    )(place, own, other)


def attend_kernel(place, tables, kv, *refs, masks, sizes, n_seq, n_qblk):
    queries, outs = refs[: len(masks)], refs[len(masks) :]
    heads, width = kv.shape[3], kv.shape[-1]
    scaling = width ** (-0.5)
    all_heads, n_vert, n_slash = sizes
    vert_cnt = all_heads * n_vert
    slash_off = vert_cnt + all_heads
    slash_cnt = slash_off + all_heads * n_slash
    key_row = lax.broadcasted_iota(jnp.int32, (BLK, BLK), 0)
    query_col = lax.broadcasted_iota(jnp.int32, (BLK, BLK), 1)
    causal = key_row <= query_col

    def place_of(block):
        span = block // n_seq
        return span % 2, (span // 2) * n_seq + block % n_seq

    def unit(query, out, slot, block):
        head = place[0] * heads + slot
        vert_live, slash_live = tables[vert_cnt + head], tables[slash_cnt + head]
        offsets = [tables[slash_off + turn * all_heads + head] for turn in range(n_slash)]
        cols, live = [block], []
        for turn, offset in enumerate(offsets):
            live.append((turn < slash_live) & (block >= offset))
            cols.append(jnp.maximum(block - offset, 0))
        for turn in range(n_vert):
            column = tables[turn * all_heads + head]
            distance = block - column
            ok = (turn < vert_live) & (distance > 0)
            for other, offset in enumerate(offsets):
                ok = ok & jnp.logical_not((other < slash_live) & (offset == distance))
            live.append(ok)
            cols.append(column)
        spots = [place_of(column) for column in cols]
        keys = jnp.concatenate([kv[side, at, 0, slot] for side, at in spots], axis=0)
        vals = jnp.concatenate([kv[side, at, 1, slot] for side, at in spots], axis=0)
        scores = lax.dot_general(
            keys, query[query.shape[0] - 1, slot], (((1,), (1,)), ((), ())), preferred_element_type=jnp.float32
        )
        parts = [jnp.where(causal, scores[:BLK], -jnp.inf)]
        for at, ok in enumerate(live):
            bias = jnp.where(ok, 0.0, -jnp.inf).astype(jnp.float32)
            parts.append(scores[(at + 1) * BLK : (at + 2) * BLK] + bias)
        top = functools.reduce(jnp.maximum, parts)
        top = jnp.max(top, axis=0, keepdims=True)
        weights = [jnp.exp((part - top) * scaling) for part in parts]
        total = jnp.sum(functools.reduce(jnp.add, weights), axis=0, keepdims=True)
        rounded = jnp.concatenate([weight.astype(jnp.bfloat16) for weight in weights], axis=0)
        acc = lax.dot_general(
            vals, rounded, (((0,), (0,)), ((), ())), preferred_element_type=jnp.float32
        )
        out[slot] = (acc / total).T.astype(jnp.bfloat16)

    @pl.loop(0, heads)
    def _(slot):
        for mask, query, out in zip(masks, queries, outs):
            unit(query, out, slot, block_of(place, mask, n_seq, n_qblk))


def attend(place, tables, sizes, kv, queries, masks):
    count = len(masks)
    _, _, _, heads, tokens, width = kv.shape
    outs = pl.pallas_call(
        functools.partial(
            attend_kernel,
            masks=masks,
            sizes=sizes,
            n_seq=lax.axis_size("seq"),
            n_qblk=lax.axis_size("qblk"),
        ),
        out_shape=[jax.ShapeDtypeStruct((heads, tokens, width), jnp.bfloat16)] * count,
        in_specs=[SMEM] * 2 + [VMEM] * (1 + count),
        out_specs=[VMEM] * count,
        compiler_params=pltpu.CompilerParams(vmem_limit_bytes=12 * MIB),
        cost_estimate=pl.CostEstimate(flops=1, bytes_accessed=1, transcendentals=0),
        name="attend",
    )(place, tables, kv, *[queries[mask] for mask in masks])
    return dict(zip(masks, outs))


def after(value, *others):
    return lax.optimization_barrier((value, *others))[0]


def group_body(queries, keys, values, *tables):
    n_seq, n_qblk = lax.axis_size("seq"), lax.axis_size("qblk")
    groups = n_seq * n_qblk
    place = jnp.stack([lax.axis_index(GROUP), lax.axis_index("sub")]).astype(jnp.int32)
    sizes = (queries.shape[2], tables[0].shape[1], tables[2].shape[1])
    flat = jnp.concatenate([table.T.reshape(-1) for table in tables])
    near, far = list(range(groups // 2)), list(range(groups // 2, groups))
    def send(part, mask, *behind):
        return swap_with(after(part, *behind) if behind else part, GROUP, mask)

    keys, values, queries = keys[0], values[0], queries[0]
    pieces = [(mask, 0, 2) for mask in far]
    kv_far = regroup(place, (keys, values), [(far, 0), (far, 1)], pieces, groups)
    takes = [(near, 0), (near, 1), (near, 2), (far, 2)]
    pieces = [(mask, 0, 3) for mask in near] + [(mask, 3, 1) for mask in far]
    rest = regroup(place, (keys, values, after(queries, flat)), takes, pieces, groups)
    got = {mask: send(kv_far[mask, 0, 2], mask) for mask in far}
    for mask in near:
        got[mask] = send(rest[mask, 0, 3], mask) if mask else rest[mask, 0, 3]
    own = gather(place, [got[mask] for mask in range(groups)])
    whole = join(place, own, swap_with(own, "sub", 1))
    arrived = {mask: got[mask] for mask in near}
    for mask in far:
        arrived[mask] = send(rest[mask, 3, 1], mask, got[mask])
    outs = attend(place, flat, sizes, whole, arrived, near)
    arrived[far[0]] = after(arrived[far[0]], outs[near[0]])
    outs.update(attend(place, flat, sizes, whole, arrived, far))
    back = {mask: send(outs[mask], mask) for mask in far}
    for mask in near:
        back[mask] = send(outs[mask], mask) if mask else outs[mask]
    begun = ungroup(place, back, near, groups)
    return ungroup(place, back, far, groups, begun)[None]


def body(queries, keys, values, *tables):
    groups, heads = lax.axis_size(GROUP), queries.shape[2]
    fits = heads % groups == 0 and heads % 32 == 0 and queries.shape[:2] == (1, BLK)
    if fits and groups & (groups - 1) == 0 and lax.axis_size("sub") == 2:
        return group_body(queries, keys, values, *tables)
    return spans_body(queries, keys, values, *tables)


def solution(mesh):
    placed = (
        P(("groups", "qblk", "sub"), "seq", None, None),
        P(("groups", "qblk", "sub"), "seq", None, None),
        P(("groups", "qblk", "sub"), "seq", None, None),
        P("groups", None),
        P("groups"),
        P("groups", None),
        P("groups"),
    )
    return jax.shard_map(
        body,
        mesh=mesh,
        in_specs=placed,
        out_specs=P(("groups", "qblk", "sub"), "seq", None, None),
        check_vma=False,
    )
```

```python
import functools

import jax
import jax.numpy as jnp
from jax import lax
from jax.experimental import pallas as pl
from jax.experimental.pallas import tpu as pltpu
from jax.sharding import PartitionSpec as P

BLK = 128


NEG_START = -1e30


def from_behind(value, axis, steps):
    count = lax.axis_size(axis)
    initial, last = (max(0, -steps), min(count, count - steps))
    return lax.ppermute(value, axis, [(source, source + steps) for source in range(initial, last)])


def pick_rows(table, chosen):
    heads = table.shape[0]
    onehot = chosen[:, None] == jnp.arange(heads, dtype=jnp.int32)[None, :]
    if table.ndim == 1:
        return jnp.sum(jnp.where(onehot, table[None, :], 0), axis=1)
    return jnp.sum(jnp.where(onehot[:, :, None], table[None, :, :], 0), axis=1)


def absorb(carry_state, scores, key_mask, tile_vals, einsum_form):
    run_max, run_sum, run_acc = carry_state
    scores = jnp.where(key_mask, scores, -jnp.inf)
    new_max = jnp.maximum(run_max, jnp.max(scores, axis=-1))
    factor = jnp.exp(run_max - new_max)
    weights = jnp.exp(scores - new_max[..., None])
    run_sum = run_sum * factor + jnp.sum(weights, axis=-1)
    run_acc = run_acc * factor[..., None] + jnp.einsum(
        einsum_form, weights.astype(jnp.bfloat16), tile_vals, preferred_element_type=jnp.float32
    )
    return (new_max, run_sum, run_acc)


def attend_head(
    q_head,
    k_head,
    v_head,
    key_prev,
    val_prev,
    sink_k,
    sink_v,
    v_list,
    v_count,
    s_list,
    s_count,
    slash_table,
    first_block,
):
    span_rows, head_width = q_head.shape
    span_blocks = span_rows // BLK
    scaling = head_width ** (-0.5)
    q_blocks = q_head.reshape(span_blocks, BLK, head_width)
    block_ids = first_block + jnp.arange(span_blocks, dtype=jnp.int32)
    carry_state = (
        jnp.full((span_blocks, BLK), NEG_START, jnp.float32),
        jnp.zeros((span_blocks, BLK), jnp.float32),
        jnp.zeros((span_blocks, BLK, head_width), jnp.float32),
    )
    k_blocks = k_head.reshape(span_blocks, BLK, head_width)
    v_blocks = v_head.reshape(span_blocks, BLK, head_width)
    scores = (
        jnp.einsum("pid,pjd->pij", q_blocks, k_blocks, preferred_element_type=jnp.float32) * scaling
    )
    causal = jnp.arange(BLK)[:, None] >= jnp.arange(BLK)[None, :]
    carry_state = absorb(carry_state, scores, causal[None], v_blocks, "pij,pjd->pid")
    ext_k = jnp.concatenate([key_prev, k_head], axis=0)
    ext_v = jnp.concatenate([val_prev, v_head], axis=0)

    def slash_step(turn_index, carry_state):
        offset = s_list[turn_index]
        start_row = span_rows - offset * BLK
        k_tile = lax.dynamic_slice_in_dim(ext_k, start_row, span_rows, 0).reshape(
            span_blocks, BLK, head_width
        )
        v_tile = lax.dynamic_slice_in_dim(ext_v, start_row, span_rows, 0).reshape(
            span_blocks, BLK, head_width
        )
        tile_scores = (
            jnp.einsum("pid,pjd->pij", q_blocks, k_tile, preferred_element_type=jnp.float32)
            * scaling
        )
        key_mask = (block_ids - offset >= 0)[:, None, None]
        return absorb(carry_state, tile_scores, key_mask, v_tile, "pij,pjd->pid")

    carry_state = lax.fori_loop(0, s_count, slash_step, carry_state)

    def vertical_step(turn_index, carry_state):
        column = v_list[turn_index]
        k_tile = sink_k[turn_index]
        v_tile = sink_v[turn_index]
        tile_scores = (
            jnp.einsum("pid,jd->pij", q_blocks, k_tile, preferred_element_type=jnp.float32)
            * scaling
        )
        distance = block_ids - column
        in_slash = (distance <= span_blocks) & slash_table[jnp.clip(distance, 0, span_blocks)]
        key_mask = ((distance > 0) & jnp.logical_not(in_slash))[:, None, None]
        return absorb(carry_state, tile_scores, key_mask, v_tile, "pij,jd->pid")

    carry_state = lax.fori_loop(0, v_count, vertical_step, carry_state)
    run_max, run_sum, run_acc = carry_state
    return (run_acc / run_sum[..., None]).astype(jnp.bfloat16).reshape(span_rows, head_width)


def spans_body(queries, keys, values, vert_idx, vert_cnt, slash_off, slash_cnt):
    n_seq = lax.axis_size("seq")
    heads = queries.shape[2]
    per_dev = heads // n_seq
    head_order = jnp.arange(heads, dtype=jnp.int32)
    q_all, k_all, v_all = (
        lax.all_to_all(queries, "seq", split_axis=2, concat_axis=1, tiled=True),
        lax.all_to_all(keys, "seq", split_axis=2, concat_axis=1, tiled=True),
        lax.all_to_all(values, "seq", split_axis=2, concat_axis=1, tiled=True),
    )
    key_prev, val_prev = from_behind((k_all, v_all), ("qblk", "sub"), 1)
    span_rows = q_all.shape[1]
    head_width = q_all.shape[3]
    span_blocks = span_rows // BLK
    first_block = lax.axis_index(("qblk", "sub")) * span_blocks
    my_heads = lax.dynamic_slice_in_dim(head_order, lax.axis_index("seq") * per_dev, per_dev)
    v_lists = pick_rows(vert_idx, my_heads)
    v_counts = pick_rows(vert_cnt, my_heads)
    s_lists = pick_rows(slash_off, my_heads)
    s_counts = pick_rows(slash_cnt, my_heads)
    local_ids = v_lists - first_block
    owned = (local_ids >= 0) & (local_ids < span_blocks)
    clipped = jnp.clip(local_ids, 0, span_blocks - 1)
    slot_ids = jnp.arange(per_dev, dtype=jnp.int32)[:, None]
    k_grid = k_all[0].reshape(span_blocks, BLK, per_dev, head_width)
    v_grid = v_all[0].reshape(span_blocks, BLK, per_dev, head_width)
    zero_half = jnp.zeros((), jnp.bfloat16)
    picked_k = jnp.where(owned[:, :, None, None], k_grid[clipped, :, slot_ids, :], zero_half)
    picked_v = jnp.where(owned[:, :, None, None], v_grid[clipped, :, slot_ids, :], zero_half)
    sink_k, sink_v = (
        lax.psum(picked_k, ("qblk", "sub")).astype(jnp.float32),
        lax.psum(picked_v, ("qblk", "sub")).astype(jnp.float32),
    )
    sink_k = sink_k.astype(jnp.bfloat16)
    sink_v = sink_v.astype(jnp.bfloat16)
    s_width = slash_off.shape[1]
    s_live = jnp.arange(s_width, dtype=jnp.int32)[None, :] < s_counts[:, None]
    offset_ids = jnp.arange(span_blocks + 1, dtype=jnp.int32)
    slash_tables = jnp.any(
        (s_lists[:, :, None] == offset_ids[None, None, :]) & s_live[:, :, None], axis=1
    )
    results = []
    for slot in range(per_dev):
        results.append(
            attend_head(
                q_all[0, :, slot, :],
                k_all[0, :, slot, :],
                v_all[0, :, slot, :],
                key_prev[0, :, slot, :],
                val_prev[0, :, slot, :],
                sink_k[slot],
                sink_v[slot],
                v_lists[slot],
                v_counts[slot],
                s_lists[slot],
                s_counts[slot],
                slash_tables[slot],
                first_block,
            )
        )
    stacked = jnp.stack(results, axis=1)[None]
    restored = lax.all_to_all(stacked, "seq", split_axis=1, concat_axis=2, tiled=True)
    return restored


GROUP = ("seq", "qblk")
MIB = 2**20
REGROUP_VMEM = 60 * MIB
RUNS = 2
CHUNKS = 4
LOG2_E = 1.4426950408889634
ANY = pl.BlockSpec(memory_space=pl.ANY)
HBM = pl.BlockSpec(memory_space=pltpu.HBM)
SMEM = pl.BlockSpec(memory_space=pltpu.SMEM)
VMEM = pl.BlockSpec(memory_space=pltpu.VMEM)


def swap_with(value, axes, mask):
    count = lax.axis_size(axes)
    return lax.ppermute(value, axes, [(source, source ^ mask) for source in range(count)])


def first_head(place, masks, heads, groups):
    half = groups // 2
    return pl.multiple_of(((place[0] ^ masks[0]) // half) * (heads // 2), heads // 2)


def regroup_kernel(place, *refs, tensors, takes, pieces, groups):
    sources, parts = refs[:tensors], refs[tensors : tensors + len(pieces)]
    staged, turned, load_sem, store_sem = refs[tensors + len(pieces) :]
    count, per_group = turned.shape[0], turned.shape[2]
    tokens, heads = sources[0].shape[:2]
    runs = [pl.ds(run * tokens // RUNS, tokens // RUNS) for run in range(RUNS)]
    loads = []
    for at, (masks, tensor) in enumerate(takes):
        first = first_head(place, masks, heads, groups)
        for into, run in enumerate(runs):
            source = sources[tensor].at[run, pl.ds(first, heads // 2)]
            loads.append(pltpu.make_async_copy(source, staged.at[at, run], load_sem.at[at, into]))
            loads[-1].start()
    stores = []
    for at in range(len(takes)):
        for into, run in enumerate(runs):
            loads[at * RUNS + into].wait()
            heads_first = jnp.swapaxes(staged[at, run], 0, 1)
            for group in range(count):
                turned[group, at, :, run] = heads_first[group * per_group : (group + 1) * per_group]
        for into, ((mask, begin, length), part) in enumerate(zip(pieces, parts)):
            if begin <= at < begin + length:
                source = turned.at[(place[0] ^ mask) % count, at]
                stores.append(
                    pltpu.make_async_copy(source, part.at[at - begin], store_sem.at[into, at - begin])
                )
                stores[-1].start()
    for store in stores:
        store.wait()


def regroup(place, tensors, takes, pieces, groups):
    tokens, heads, width = tensors[0].shape
    part = (heads // groups, tokens, width)
    parts = pl.pallas_call(
        functools.partial(
            regroup_kernel, tensors=len(tensors), takes=takes, pieces=pieces, groups=groups
        ),
        out_shape=[
            jax.ShapeDtypeStruct((length,) + part, jnp.bfloat16) for _, _, length in pieces
        ],
        in_specs=[SMEM] + [HBM] * len(tensors),
        out_specs=[ANY] * len(pieces),
        scratch_shapes=[
            pltpu.VMEM((len(takes), tokens, heads // 2, width), jnp.bfloat16),
            pltpu.VMEM((groups // 2, len(takes)) + part, jnp.bfloat16),
            pltpu.SemaphoreType.DMA((len(takes), RUNS)),
            pltpu.SemaphoreType.DMA((len(pieces), len(takes))),
        ],
        compiler_params=pltpu.CompilerParams(vmem_limit_bytes=REGROUP_VMEM),
        cost_estimate=pl.CostEstimate(flops=1, bytes_accessed=1, transcendentals=0),
        name="regroup",
    )(place, *tensors)
    return dict(zip(pieces, parts))


def ungroup_kernel(place, *refs, masks, groups):
    parts = refs[: len(masks)]
    out, staged, turned, store_sem = refs[-4:]
    count, per_group, _, width = staged.shape
    tokens, heads = out.shape[:2]
    first = first_head(place, masks, heads, groups)
    for part, mask in zip(parts, masks):
        staged[(place[0] ^ mask) % count] = part[...]
    stores = []
    for chunk in range(CHUNKS):
        run = pl.ds(chunk * tokens // CHUNKS, tokens // CHUNKS)
        heads_first = staged[:, :, run].reshape(count * per_group, tokens // CHUNKS, width)
        turned[run] = jnp.swapaxes(heads_first, 0, 1)
        target = out.at[run, pl.ds(first, heads // 2)]
        stores.append(pltpu.make_async_copy(turned.at[run], target, store_sem.at[chunk]))
        stores[-1].start()
    for store in stores:
        store.wait()


def ungroup(place, parts, masks, groups, begun=None):
    per_group, tokens, width = parts[masks[0]].shape
    shape = (tokens, groups * per_group, width)
    return pl.pallas_call(
        functools.partial(ungroup_kernel, masks=masks, groups=groups),
        out_shape=jax.ShapeDtypeStruct(shape, jnp.bfloat16),
        in_specs=[SMEM] + [VMEM] * len(masks) + ([] if begun is None else [HBM]),
        out_specs=HBM,
        scratch_shapes=[
            pltpu.VMEM((len(masks), per_group, tokens, width), jnp.bfloat16),
            pltpu.VMEM((tokens, len(masks) * per_group, width), jnp.bfloat16),
            pltpu.SemaphoreType.DMA((CHUNKS,)),
        ],
        input_output_aliases={} if begun is None else {1 + len(masks): 0},
        compiler_params=pltpu.CompilerParams(vmem_limit_bytes=6 * MIB),
        cost_estimate=pl.CostEstimate(flops=1, bytes_accessed=1, transcendentals=0),
        name="ungroup",
    )(place, *[parts[mask] for mask in masks], *([] if begun is None else [begun]))


def block_of(place, mask, n_seq, n_qblk):
    partner = place[0] ^ mask
    return (2 * (partner % n_qblk) + place[1]) * n_seq + partner // n_qblk


def gather_kernel(place, *refs, groups, n_seq, n_qblk):
    own, out, sem = refs[:groups], refs[groups], refs[groups + 1]
    copies = [
        pltpu.make_async_copy(
            part.at[pl.ds(0, 2)],
            out.at[((place[0] ^ mask) % n_qblk) * n_seq + (place[0] ^ mask) // n_qblk],
            sem.at[mask],
        )
        for mask, part in enumerate(own)
    ]
    for copy in copies:
        copy.start()
    for copy in copies:
        copy.wait()


def gather(place, parts):
    groups = len(parts)
    shape = (groups, 2) + parts[0].shape[1:]
    return pl.pallas_call(
        functools.partial(
            gather_kernel,
            groups=groups,
            n_seq=lax.axis_size("seq"),
            n_qblk=lax.axis_size("qblk"),
        ),
        out_shape=jax.ShapeDtypeStruct(shape, jnp.bfloat16),
        in_specs=[SMEM] + [ANY] * groups,
        out_specs=ANY,
        scratch_shapes=[pltpu.SemaphoreType.DMA((groups,))],
        compiler_params=pltpu.CompilerParams(vmem_limit_bytes=2 * MIB),
        cost_estimate=pl.CostEstimate(flops=1, bytes_accessed=1, transcendentals=0),
        name="gather",
    )(place, *parts)


def attend_kernel(place, tables, *refs, masks, sizes, n_seq, n_qblk, sides):
    count = len(masks)
    loads = []
    if sides:
        sides, queries, outs = refs[:2], refs[2 : 2 + count], refs[2 + count : 2 + 2 * count]
        kv, sem = refs[-2:]
        for slot in range(kv.shape[0]):
            for at, side in enumerate(sides):
                target = kv.at[slot, place[1] ^ at]
                loads.append(pltpu.make_async_copy(side.at[:, :, slot], target, sem.at[slot, at]))
                loads[-1].start()
    else:
        kv, queries, outs = refs[0], refs[1 : 1 + count], refs[1 + count :]
    heads, width = kv.shape[0], kv.shape[-1]
    scaling = width ** (-0.5) * LOG2_E
    all_heads, n_vert, n_slash = sizes
    vert_cnt = all_heads * n_vert
    slash_off = vert_cnt + all_heads
    slash_cnt = slash_off + all_heads * n_slash
    key_row = lax.broadcasted_iota(jnp.int32, (BLK, BLK), 0)
    query_col = lax.broadcasted_iota(jnp.int32, (BLK, BLK), 1)
    causal = key_row <= query_col

    def tile(block, tensor, slot):
        span = block // n_seq
        return kv[slot, span % 2, (span // 2) * n_seq + block % n_seq, tensor]

    def unit(query, out, slot, block):
        head = place[0] * heads + slot
        vert_live, slash_live = tables[vert_cnt + head], tables[slash_cnt + head]
        offsets = [tables[slash_off + turn * all_heads + head] for turn in range(n_slash)]
        cols, live = [block], []
        for turn, offset in enumerate(offsets):
            live.append((turn < slash_live) & (block >= offset))
            cols.append(jnp.maximum(block - offset, 0))
        for turn in range(n_vert):
            column = tables[turn * all_heads + head]
            distance = block - column
            ok = (turn < vert_live) & (distance > 0)
            for other, offset in enumerate(offsets):
                ok = ok & jnp.logical_not((other < slash_live) & (offset == distance))
            live.append(ok)
            cols.append(column)
        keys = jnp.concatenate([tile(column, 0, slot) for column in cols], axis=0)
        vals = jnp.concatenate([tile(column, 1, slot) for column in cols], axis=0)
        scores = lax.dot_general(
            keys, query[query.shape[0] - 1, slot], (((1,), (1,)), ((), ())), preferred_element_type=jnp.float32
        )
        parts = [jnp.where(causal, scores[:BLK], -jnp.inf)]
        for at, ok in enumerate(live):
            bias = jnp.where(ok, 0.0, -jnp.inf).astype(jnp.float32)
            parts.append(scores[(at + 1) * BLK : (at + 2) * BLK] + bias)
        top = functools.reduce(jnp.maximum, parts)
        top = jnp.max(top, axis=0, keepdims=True)
        weights = [jnp.exp2((part - top) * scaling) for part in parts]
        total = jnp.sum(functools.reduce(jnp.add, weights), axis=0, keepdims=True)
        rounded = jnp.concatenate([weight.astype(jnp.bfloat16) for weight in weights], axis=0)
        acc = lax.dot_general(
            vals, rounded, (((0,), (0,)), ((), ())), preferred_element_type=jnp.float32
        )
        out[slot] = (acc * (1.0 / total)).T.astype(jnp.bfloat16)

    for slot in range(heads):
        for load in loads[2 * slot : 2 * slot + 2]:
            load.wait()
        for mask, query, out in zip(masks, queries, outs):
            unit(query, out, slot, block_of(place, mask, n_seq, n_qblk))


def attend(place, tables, sizes, kv, queries, masks):
    sides, count = isinstance(kv, (tuple, list)), len(masks)
    if sides:
        spots, _, heads, tokens, width = kv[0].shape
        whole = jax.ShapeDtypeStruct((heads, 2, spots, 2, tokens, width), jnp.bfloat16)
    else:
        heads, _, _, _, tokens, width = kv.shape
    outs = pl.pallas_call(
        functools.partial(
            attend_kernel,
            masks=masks,
            sizes=sizes,
            n_seq=lax.axis_size("seq"),
            n_qblk=lax.axis_size("qblk"),
            sides=sides,
        ),
        out_shape=[jax.ShapeDtypeStruct((heads, tokens, width), jnp.bfloat16)] * count
        + ([whole] if sides else []),
        in_specs=[SMEM] * 2 + ([ANY] * 2 if sides else [VMEM]) + [VMEM] * count,
        out_specs=[VMEM] * (count + sides),
        scratch_shapes=[pltpu.SemaphoreType.DMA((heads, 2))] if sides else [],
        compiler_params=pltpu.CompilerParams(vmem_limit_bytes=12 * MIB),
        cost_estimate=pl.CostEstimate(flops=1, bytes_accessed=1, transcendentals=0),
        name="attend",
    )(place, tables, *(kv if sides else [kv]), *[queries[mask] for mask in masks])
    return dict(zip(masks, outs)), (outs[-1] if sides else kv)


def after(value, *others):
    return lax.optimization_barrier((value, *others))[0]


def group_body(queries, keys, values, *tables):
    n_seq, n_qblk = lax.axis_size("seq"), lax.axis_size("qblk")
    groups = n_seq * n_qblk
    place = jnp.stack([lax.axis_index(GROUP), lax.axis_index("sub")]).astype(jnp.int32)
    sizes = (queries.shape[2], tables[0].shape[1], tables[2].shape[1])
    flat = jnp.concatenate([table.T.reshape(-1) for table in tables])
    near, far = list(range(groups // 2)), list(range(groups // 2, groups))
    def send(part, mask, *behind):
        return swap_with(after(part, *behind) if behind else part, GROUP, mask)

    keys, values, queries = keys[0], values[0], queries[0]
    pieces = [(mask, 0, 2) for mask in far]
    kv_far = regroup(place, (keys, values), [(far, 0), (far, 1)], pieces, groups)
    takes = [(near, 0), (near, 1), (near, 2), (far, 2)]
    pieces = [(mask, 0, 3) for mask in near] + [(mask, 3, 1) for mask in far]
    rest = regroup(place, (keys, values, after(queries, flat)), takes, pieces, groups)
    got = {mask: send(kv_far[mask, 0, 2], mask) for mask in far}
    for mask in near:
        got[mask] = send(rest[mask, 0, 3], mask) if mask else rest[mask, 0, 3]
    def share(*parts):
        own = gather(place, parts)
        return own, swap_with(own, "sub", 1)

    def share_again(*parts):
        own = gather(place, parts)
        return own, swap_with(after(own, place), "sub", 1)

    some = tables[1][0] >= 1
    sides = lax.cond(some, share, share_again, *[got[mask] for mask in range(groups)])
    arrived = {mask: got[mask] for mask in near}
    for mask in far:
        arrived[mask] = send(rest[mask, 3, 1], mask)
    outs, kv = attend(place, flat, sizes, sides, arrived, near)
    outs.update(attend(place, flat, sizes, kv, arrived, far)[0])
    back = {mask: send(outs[mask], mask) for mask in far}
    for mask in near:
        back[mask] = send(outs[mask], mask) if mask else outs[mask]
    begun = ungroup(place, back, near, groups)
    return ungroup(place, back, far, groups, begun)[None]


def body(queries, keys, values, *tables):
    groups, heads = lax.axis_size(GROUP), queries.shape[2]
    fits = heads % groups == 0 and heads % 32 == 0 and queries.shape[:2] == (1, BLK)
    if fits and groups & (groups - 1) == 0 and lax.axis_size("sub") == 2:
        return group_body(queries, keys, values, *tables)
    return spans_body(queries, keys, values, *tables)


def solution(mesh):
    placed = (
        P(("groups", "qblk", "sub"), "seq", None, None),
        P(("groups", "qblk", "sub"), "seq", None, None),
        P(("groups", "qblk", "sub"), "seq", None, None),
        P("groups", None),
        P("groups"),
        P("groups", None),
        P("groups"),
    )
    return jax.shard_map(
        body,
        mesh=mesh,
        in_specs=placed,
        out_specs=P(("groups", "qblk", "sub"), "seq", None, None),
        check_vma=False,
    )
```

```python
import functools

import jax
import jax.numpy as jnp
from jax import lax
from jax.experimental import pallas as pl
from jax.experimental.pallas import tpu as pltpu
from jax.sharding import PartitionSpec as P

BLK = 128


NEG_START = -1e30


def from_behind(value, axis, steps):
    count = lax.axis_size(axis)
    initial, last = (max(0, -steps), min(count, count - steps))
    return lax.ppermute(value, axis, [(source, source + steps) for source in range(initial, last)])


def pick_rows(table, chosen):
    heads = table.shape[0]
    onehot = chosen[:, None] == jnp.arange(heads, dtype=jnp.int32)[None, :]
    if table.ndim == 1:
        return jnp.sum(jnp.where(onehot, table[None, :], 0), axis=1)
    return jnp.sum(jnp.where(onehot[:, :, None], table[None, :, :], 0), axis=1)


def absorb(carry_state, scores, key_mask, tile_vals, einsum_form):
    run_max, run_sum, run_acc = carry_state
    scores = jnp.where(key_mask, scores, -jnp.inf)
    new_max = jnp.maximum(run_max, jnp.max(scores, axis=-1))
    factor = jnp.exp(run_max - new_max)
    weights = jnp.exp(scores - new_max[..., None])
    run_sum = run_sum * factor + jnp.sum(weights, axis=-1)
    run_acc = run_acc * factor[..., None] + jnp.einsum(
        einsum_form, weights.astype(jnp.bfloat16), tile_vals, preferred_element_type=jnp.float32
    )
    return (new_max, run_sum, run_acc)


def attend_head(
    q_head,
    k_head,
    v_head,
    key_prev,
    val_prev,
    sink_k,
    sink_v,
    v_list,
    v_count,
    s_list,
    s_count,
    slash_table,
    first_block,
):
    span_rows, head_width = q_head.shape
    span_blocks = span_rows // BLK
    scaling = head_width ** (-0.5)
    q_blocks = q_head.reshape(span_blocks, BLK, head_width)
    block_ids = first_block + jnp.arange(span_blocks, dtype=jnp.int32)
    carry_state = (
        jnp.full((span_blocks, BLK), NEG_START, jnp.float32),
        jnp.zeros((span_blocks, BLK), jnp.float32),
        jnp.zeros((span_blocks, BLK, head_width), jnp.float32),
    )
    k_blocks = k_head.reshape(span_blocks, BLK, head_width)
    v_blocks = v_head.reshape(span_blocks, BLK, head_width)
    scores = (
        jnp.einsum("pid,pjd->pij", q_blocks, k_blocks, preferred_element_type=jnp.float32) * scaling
    )
    causal = jnp.arange(BLK)[:, None] >= jnp.arange(BLK)[None, :]
    carry_state = absorb(carry_state, scores, causal[None], v_blocks, "pij,pjd->pid")
    ext_k = jnp.concatenate([key_prev, k_head], axis=0)
    ext_v = jnp.concatenate([val_prev, v_head], axis=0)

    def slash_step(turn_index, carry_state):
        offset = s_list[turn_index]
        start_row = span_rows - offset * BLK
        k_tile = lax.dynamic_slice_in_dim(ext_k, start_row, span_rows, 0).reshape(
            span_blocks, BLK, head_width
        )
        v_tile = lax.dynamic_slice_in_dim(ext_v, start_row, span_rows, 0).reshape(
            span_blocks, BLK, head_width
        )
        tile_scores = (
            jnp.einsum("pid,pjd->pij", q_blocks, k_tile, preferred_element_type=jnp.float32)
            * scaling
        )
        key_mask = (block_ids - offset >= 0)[:, None, None]
        return absorb(carry_state, tile_scores, key_mask, v_tile, "pij,pjd->pid")

    carry_state = lax.fori_loop(0, s_count, slash_step, carry_state)

    def vertical_step(turn_index, carry_state):
        column = v_list[turn_index]
        k_tile = sink_k[turn_index]
        v_tile = sink_v[turn_index]
        tile_scores = (
            jnp.einsum("pid,jd->pij", q_blocks, k_tile, preferred_element_type=jnp.float32)
            * scaling
        )
        distance = block_ids - column
        in_slash = (distance <= span_blocks) & slash_table[jnp.clip(distance, 0, span_blocks)]
        key_mask = ((distance > 0) & jnp.logical_not(in_slash))[:, None, None]
        return absorb(carry_state, tile_scores, key_mask, v_tile, "pij,jd->pid")

    carry_state = lax.fori_loop(0, v_count, vertical_step, carry_state)
    run_max, run_sum, run_acc = carry_state
    return (run_acc / run_sum[..., None]).astype(jnp.bfloat16).reshape(span_rows, head_width)


def spans_body(queries, keys, values, vert_idx, vert_cnt, slash_off, slash_cnt):
    n_seq = lax.axis_size("seq")
    heads = queries.shape[2]
    per_dev = heads // n_seq
    head_order = jnp.arange(heads, dtype=jnp.int32)
    q_all, k_all, v_all = (
        lax.all_to_all(queries, "seq", split_axis=2, concat_axis=1, tiled=True),
        lax.all_to_all(keys, "seq", split_axis=2, concat_axis=1, tiled=True),
        lax.all_to_all(values, "seq", split_axis=2, concat_axis=1, tiled=True),
    )
    key_prev, val_prev = from_behind((k_all, v_all), ("qblk", "sub"), 1)
    span_rows = q_all.shape[1]
    head_width = q_all.shape[3]
    span_blocks = span_rows // BLK
    first_block = lax.axis_index(("qblk", "sub")) * span_blocks
    my_heads = lax.dynamic_slice_in_dim(head_order, lax.axis_index("seq") * per_dev, per_dev)
    v_lists = pick_rows(vert_idx, my_heads)
    v_counts = pick_rows(vert_cnt, my_heads)
    s_lists = pick_rows(slash_off, my_heads)
    s_counts = pick_rows(slash_cnt, my_heads)
    local_ids = v_lists - first_block
    owned = (local_ids >= 0) & (local_ids < span_blocks)
    clipped = jnp.clip(local_ids, 0, span_blocks - 1)
    slot_ids = jnp.arange(per_dev, dtype=jnp.int32)[:, None]
    k_grid = k_all[0].reshape(span_blocks, BLK, per_dev, head_width)
    v_grid = v_all[0].reshape(span_blocks, BLK, per_dev, head_width)
    zero_half = jnp.zeros((), jnp.bfloat16)
    picked_k = jnp.where(owned[:, :, None, None], k_grid[clipped, :, slot_ids, :], zero_half)
    picked_v = jnp.where(owned[:, :, None, None], v_grid[clipped, :, slot_ids, :], zero_half)
    sink_k, sink_v = (
        lax.psum(picked_k, ("qblk", "sub")).astype(jnp.float32),
        lax.psum(picked_v, ("qblk", "sub")).astype(jnp.float32),
    )
    sink_k = sink_k.astype(jnp.bfloat16)
    sink_v = sink_v.astype(jnp.bfloat16)
    s_width = slash_off.shape[1]
    s_live = jnp.arange(s_width, dtype=jnp.int32)[None, :] < s_counts[:, None]
    offset_ids = jnp.arange(span_blocks + 1, dtype=jnp.int32)
    slash_tables = jnp.any(
        (s_lists[:, :, None] == offset_ids[None, None, :]) & s_live[:, :, None], axis=1
    )
    results = []
    for slot in range(per_dev):
        results.append(
            attend_head(
                q_all[0, :, slot, :],
                k_all[0, :, slot, :],
                v_all[0, :, slot, :],
                key_prev[0, :, slot, :],
                val_prev[0, :, slot, :],
                sink_k[slot],
                sink_v[slot],
                v_lists[slot],
                v_counts[slot],
                s_lists[slot],
                s_counts[slot],
                slash_tables[slot],
                first_block,
            )
        )
    stacked = jnp.stack(results, axis=1)[None]
    restored = lax.all_to_all(stacked, "seq", split_axis=1, concat_axis=2, tiled=True)
    return restored


GROUP = ("seq", "qblk")
MIB = 2**20
REGROUP_VMEM = 60 * MIB
RUNS = 2
CHUNKS = 4
LOG2_E = 1.4426950408889634
ANY = pl.BlockSpec(memory_space=pl.ANY)
HBM = pl.BlockSpec(memory_space=pltpu.HBM)
SMEM = pl.BlockSpec(memory_space=pltpu.SMEM)
VMEM = pl.BlockSpec(memory_space=pltpu.VMEM)


def swap_with(value, axes, mask):
    count = lax.axis_size(axes)
    return lax.ppermute(value, axes, [(source, source ^ mask) for source in range(count)])


def first_head(place, masks, heads, groups):
    half = groups // 2
    return pl.multiple_of(((place[0] ^ masks[0]) // half) * (heads // 2), heads // 2)


def regroup_kernel(place, *refs, tensors, takes, pieces, groups):
    sources, parts = refs[:tensors], refs[tensors : tensors + len(pieces)]
    staged, turned, load_sem, store_sem = refs[tensors + len(pieces) :]
    count, per_group = turned.shape[0], turned.shape[2]
    tokens, heads = sources[0].shape[:2]
    runs = [pl.ds(run * tokens // RUNS, tokens // RUNS) for run in range(RUNS)]
    loads = []
    for at, (masks, tensor) in enumerate(takes):
        first = first_head(place, masks, heads, groups)
        for into, run in enumerate(runs):
            source = sources[tensor].at[run, pl.ds(first, heads // 2)]
            loads.append(pltpu.make_async_copy(source, staged.at[at, run], load_sem.at[at, into]))
            loads[-1].start()
    stores = []
    for at in range(len(takes)):
        for into, run in enumerate(runs):
            loads[at * RUNS + into].wait()
            heads_first = jnp.swapaxes(staged[at, run], 0, 1)
            for group in range(count):
                turned[group, at, :, run] = heads_first[group * per_group : (group + 1) * per_group]
        for into, ((mask, begin, length), part) in enumerate(zip(pieces, parts)):
            if begin <= at < begin + length:
                source = turned.at[(place[0] ^ mask) % count, at]
                stores.append(
                    pltpu.make_async_copy(source, part.at[at - begin], store_sem.at[into, at - begin])
                )
                stores[-1].start()
    for store in stores:
        store.wait()


def regroup(place, tensors, takes, pieces, groups):
    tokens, heads, width = tensors[0].shape
    part = (heads // groups, tokens, width)
    parts = pl.pallas_call(
        functools.partial(
            regroup_kernel, tensors=len(tensors), takes=takes, pieces=pieces, groups=groups
        ),
        out_shape=[
            jax.ShapeDtypeStruct((length,) + part, jnp.bfloat16) for _, _, length in pieces
        ],
        in_specs=[SMEM] + [HBM] * len(tensors),
        out_specs=[ANY] * len(pieces),
        scratch_shapes=[
            pltpu.VMEM((len(takes), tokens, heads // 2, width), jnp.bfloat16),
            pltpu.VMEM((groups // 2, len(takes)) + part, jnp.bfloat16),
            pltpu.SemaphoreType.DMA((len(takes), RUNS)),
            pltpu.SemaphoreType.DMA((len(pieces), len(takes))),
        ],
        compiler_params=pltpu.CompilerParams(vmem_limit_bytes=REGROUP_VMEM),
        cost_estimate=pl.CostEstimate(flops=1, bytes_accessed=1, transcendentals=0),
        name="regroup",
    )(place, *tensors)
    return dict(zip(pieces, parts))


def ungroup_kernel(place, *refs, masks, groups):
    parts = refs[: len(masks)]
    out, staged, turned, store_sem = refs[-4:]
    count, per_group, _, width = staged.shape
    tokens, heads = out.shape[:2]
    first = first_head(place, masks, heads, groups)
    for part, mask in zip(parts, masks):
        staged[(place[0] ^ mask) % count] = part[...]
    stores = []
    for chunk in range(CHUNKS):
        run = pl.ds(chunk * tokens // CHUNKS, tokens // CHUNKS)
        heads_first = staged[:, :, run].reshape(count * per_group, tokens // CHUNKS, width)
        turned[run] = jnp.swapaxes(heads_first, 0, 1)
        target = out.at[run, pl.ds(first, heads // 2)]
        stores.append(pltpu.make_async_copy(turned.at[run], target, store_sem.at[chunk]))
        stores[-1].start()
    for store in stores:
        store.wait()


def ungroup(place, parts, masks, groups, begun=None):
    per_group, tokens, width = parts[masks[0]].shape
    shape = (tokens, groups * per_group, width)
    return pl.pallas_call(
        functools.partial(ungroup_kernel, masks=masks, groups=groups),
        out_shape=jax.ShapeDtypeStruct(shape, jnp.bfloat16),
        in_specs=[SMEM] + [VMEM] * len(masks) + ([] if begun is None else [HBM]),
        out_specs=HBM,
        scratch_shapes=[
            pltpu.VMEM((len(masks), per_group, tokens, width), jnp.bfloat16),
            pltpu.VMEM((tokens, len(masks) * per_group, width), jnp.bfloat16),
            pltpu.SemaphoreType.DMA((CHUNKS,)),
        ],
        input_output_aliases={} if begun is None else {1 + len(masks): 0},
        compiler_params=pltpu.CompilerParams(vmem_limit_bytes=6 * MIB),
        cost_estimate=pl.CostEstimate(flops=1, bytes_accessed=1, transcendentals=0),
        name="ungroup",
    )(place, *[parts[mask] for mask in masks], *([] if begun is None else [begun]))


def block_of(place, mask, n_seq, n_qblk):
    partner = place[0] ^ mask
    return (2 * (partner % n_qblk) + place[1]) * n_seq + partner // n_qblk


def gather_kernel(place, *refs, groups, n_seq, n_qblk):
    own, out, sem = refs[:groups], refs[groups], refs[groups + 1]
    copies = [
        pltpu.make_async_copy(
            part.at[pl.ds(0, 2)],
            out.at[((place[0] ^ mask) % n_qblk) * n_seq + (place[0] ^ mask) // n_qblk],
            sem.at[mask],
        )
        for mask, part in enumerate(own)
    ]
    for copy in copies:
        copy.start()
    for copy in copies:
        copy.wait()


def gather(place, parts):
    groups = len(parts)
    shape = (groups, 2) + parts[0].shape[1:]
    return pl.pallas_call(
        functools.partial(
            gather_kernel,
            groups=groups,
            n_seq=lax.axis_size("seq"),
            n_qblk=lax.axis_size("qblk"),
        ),
        out_shape=jax.ShapeDtypeStruct(shape, jnp.bfloat16),
        in_specs=[SMEM] + [ANY] * groups,
        out_specs=ANY,
        scratch_shapes=[pltpu.SemaphoreType.DMA((groups,))],
        compiler_params=pltpu.CompilerParams(vmem_limit_bytes=2 * MIB),
        cost_estimate=pl.CostEstimate(flops=1, bytes_accessed=1, transcendentals=0),
        name="gather",
    )(place, *parts)


def attend_kernel(place, tables, *refs, masks, sizes, n_seq, n_qblk, sides):
    count = len(masks)
    loads = []
    if sides:
        sides, queries, outs = refs[:2], refs[2 : 2 + count], refs[2 + count : 2 + 2 * count]
        kv, sem = refs[-2:]
        for slot in range(kv.shape[0]):
            for at, side in enumerate(sides):
                target = kv.at[slot, place[1] ^ at]
                loads.append(pltpu.make_async_copy(side.at[:, :, slot], target, sem.at[slot, at]))
                loads[-1].start()
    else:
        kv, queries, outs = refs[0], refs[1 : 1 + count], refs[1 + count :]
    heads, width = kv.shape[0], kv.shape[-1]
    scaling = width ** (-0.5) * LOG2_E
    all_heads, n_vert, n_slash = sizes
    vert_cnt = all_heads * n_vert
    slash_off = vert_cnt + all_heads
    slash_cnt = slash_off + all_heads * n_slash
    key_row = lax.broadcasted_iota(jnp.int32, (BLK, BLK), 0)
    query_col = lax.broadcasted_iota(jnp.int32, (BLK, BLK), 1)
    causal = key_row <= query_col

    def tile(block, tensor, slot):
        span = block // n_seq
        return kv[slot, span % 2, (span // 2) * n_seq + block % n_seq, tensor]

    def unit(query, out, slot, block):
        head = place[0] * heads + slot
        vert_live, slash_live = tables[vert_cnt + head], tables[slash_cnt + head]
        offsets = [tables[slash_off + turn * all_heads + head] for turn in range(n_slash)]
        cols, live = [block], []
        for turn, offset in enumerate(offsets):
            live.append((turn < slash_live) & (block >= offset))
            cols.append(jnp.maximum(block - offset, 0))
        for turn in range(n_vert):
            column = tables[turn * all_heads + head]
            distance = block - column
            ok = (turn < vert_live) & (distance > 0)
            for other, offset in enumerate(offsets):
                ok = ok & jnp.logical_not((other < slash_live) & (offset == distance))
            live.append(ok)
            cols.append(column)
        keys = jnp.concatenate([tile(column, 0, slot) for column in cols], axis=0)
        vals = jnp.concatenate([tile(column, 1, slot) for column in cols], axis=0)
        scores = lax.dot_general(
            keys, query[query.shape[0] - 1, slot], (((1,), (1,)), ((), ())), preferred_element_type=jnp.float32
        )
        parts = [jnp.where(causal, scores[:BLK], -jnp.inf)]
        for at, ok in enumerate(live):
            bias = jnp.where(ok, 0.0, -jnp.inf).astype(jnp.float32)
            parts.append(scores[(at + 1) * BLK : (at + 2) * BLK] + bias)
        top = functools.reduce(jnp.maximum, parts)
        top = jnp.max(top, axis=0, keepdims=True)
        weights = [jnp.exp2((part - top) * scaling) for part in parts]
        total = jnp.sum(functools.reduce(jnp.add, weights), axis=0, keepdims=True)
        rounded = jnp.concatenate([weight.astype(jnp.bfloat16) for weight in weights], axis=0)
        acc = lax.dot_general(
            vals, rounded, (((0,), (0,)), ((), ())), preferred_element_type=jnp.float32
        )
        out[slot] = (acc * (1.0 / total)).T.astype(jnp.bfloat16)

    for slot in range(heads):
        for load in loads[2 * slot : 2 * slot + 2]:
            load.wait()
        for mask, query, out in zip(masks, queries, outs):
            unit(query, out, slot, block_of(place, mask, n_seq, n_qblk))


def attend(place, tables, sizes, kv, queries, masks):
    sides, count = isinstance(kv, (tuple, list)), len(masks)
    if sides:
        spots, _, heads, tokens, width = kv[0].shape
        whole = jax.ShapeDtypeStruct((heads, 2, spots, 2, tokens, width), jnp.bfloat16)
    else:
        heads, _, _, _, tokens, width = kv.shape
    outs = pl.pallas_call(
        functools.partial(
            attend_kernel,
            masks=masks,
            sizes=sizes,
            n_seq=lax.axis_size("seq"),
            n_qblk=lax.axis_size("qblk"),
            sides=sides,
        ),
        out_shape=[jax.ShapeDtypeStruct((heads, tokens, width), jnp.bfloat16)] * count
        + ([whole] if sides else []),
        in_specs=[SMEM] * 2 + ([ANY] * 2 if sides else [VMEM]) + [VMEM] * count,
        out_specs=[VMEM] * (count + sides),
        scratch_shapes=[pltpu.SemaphoreType.DMA((heads, 2))] if sides else [],
        compiler_params=pltpu.CompilerParams(vmem_limit_bytes=12 * MIB),
        cost_estimate=pl.CostEstimate(flops=1, bytes_accessed=1, transcendentals=0),
        name="attend",
    )(place, tables, *(kv if sides else [kv]), *[queries[mask] for mask in masks])
    return dict(zip(masks, outs)), (outs[-1] if sides else kv)


def after(value, *others):
    return lax.optimization_barrier((value, *others))[0]


def group_body(queries, keys, values, *tables):
    n_seq, n_qblk = lax.axis_size("seq"), lax.axis_size("qblk")
    groups = n_seq * n_qblk
    place = jnp.stack([lax.axis_index(GROUP), lax.axis_index("sub")]).astype(jnp.int32)
    sizes = (queries.shape[2], tables[0].shape[1], tables[2].shape[1])
    flat = jnp.concatenate([table.T.reshape(-1) for table in tables])
    near, far = list(range(groups // 2)), list(range(groups // 2, groups))
    def send(part, mask):
        return swap_with(part, GROUP, mask) if mask else part

    keys, values, queries = keys[0], values[0], queries[0]
    pieces = [(mask, 0, 2) for mask in far]
    kv_far = regroup(place, (keys, values), [(far, 0), (far, 1)], pieces, groups)
    takes = [(near, 0), (near, 1), (near, 2), (far, 2)]
    pieces = [(mask, 0, 3) for mask in near] + [(mask, 3, 1) for mask in far]
    rest = regroup(place, (keys, values, after(queries, flat)), takes, pieces, groups)
    got = {mask: send(rest[mask, 0, 3], mask) for mask in near}
    got.update({mask: send(kv_far[mask, 0, 2], mask) for mask in far})

    def share(*parts):
        own = gather(place, parts)
        return own, swap_with(own, "sub", 1)

    def share_again(*parts):
        own = gather(place, parts)
        return own, swap_with(after(own, place), "sub", 1)

    some = tables[1][0] >= 1
    sides = lax.cond(some, share, share_again, *[got[mask] for mask in range(groups)])
    arrived = {mask: got[mask] for mask in near}
    arrived.update({mask: send(rest[mask, 3, 1], mask) for mask in far})
    cut = len(far) // 2
    outs, kv = attend(place, flat, sizes, sides, arrived, near + far[:cut])
    outs.update(attend(place, flat, sizes, kv, arrived, far[cut:])[0])
    back = {mask: send(outs[mask], mask) for mask in near}
    back.update({mask: send(outs[mask], mask) for mask in far})
    begun = ungroup(place, back, near, groups)
    return ungroup(place, back, far, groups, begun)[None]


def body(queries, keys, values, *tables):
    groups, heads = lax.axis_size(GROUP), queries.shape[2]
    fits = heads % groups == 0 and heads % 32 == 0 and queries.shape[:2] == (1, BLK)
    if fits and groups & (groups - 1) == 0 and lax.axis_size("sub") == 2:
        return group_body(queries, keys, values, *tables)
    return spans_body(queries, keys, values, *tables)


def solution(mesh):
    placed = (
        P(("groups", "qblk", "sub"), "seq", None, None),
        P(("groups", "qblk", "sub"), "seq", None, None),
        P(("groups", "qblk", "sub"), "seq", None, None),
        P("groups", None),
        P("groups"),
        P("groups", None),
        P("groups"),
    )
    return jax.shard_map(
        body,
        mesh=mesh,
        in_specs=placed,
        out_specs=P(("groups", "qblk", "sub"), "seq", None, None),
        check_vma=False,
    )
```

```python
import functools

import jax
import jax.numpy as jnp
from jax import lax
from jax.experimental import pallas as pl
from jax.experimental.pallas import tpu as pltpu
from jax.sharding import PartitionSpec as P

BLK = 128


NEG_START = -1e30


def from_behind(value, axis, steps):
    count = lax.axis_size(axis)
    initial, last = (max(0, -steps), min(count, count - steps))
    return lax.ppermute(value, axis, [(source, source + steps) for source in range(initial, last)])


def pick_rows(table, chosen):
    heads = table.shape[0]
    onehot = chosen[:, None] == jnp.arange(heads, dtype=jnp.int32)[None, :]
    if table.ndim == 1:
        return jnp.sum(jnp.where(onehot, table[None, :], 0), axis=1)
    return jnp.sum(jnp.where(onehot[:, :, None], table[None, :, :], 0), axis=1)


def absorb(carry_state, scores, key_mask, tile_vals, einsum_form):
    run_max, run_sum, run_acc = carry_state
    scores = jnp.where(key_mask, scores, -jnp.inf)
    new_max = jnp.maximum(run_max, jnp.max(scores, axis=-1))
    factor = jnp.exp(run_max - new_max)
    weights = jnp.exp(scores - new_max[..., None])
    run_sum = run_sum * factor + jnp.sum(weights, axis=-1)
    run_acc = run_acc * factor[..., None] + jnp.einsum(
        einsum_form, weights.astype(jnp.bfloat16), tile_vals, preferred_element_type=jnp.float32
    )
    return (new_max, run_sum, run_acc)


def attend_head(
    q_head,
    k_head,
    v_head,
    key_prev,
    val_prev,
    sink_k,
    sink_v,
    v_list,
    v_count,
    s_list,
    s_count,
    slash_table,
    first_block,
):
    span_rows, head_width = q_head.shape
    span_blocks = span_rows // BLK
    scaling = head_width ** (-0.5)
    q_blocks = q_head.reshape(span_blocks, BLK, head_width)
    block_ids = first_block + jnp.arange(span_blocks, dtype=jnp.int32)
    carry_state = (
        jnp.full((span_blocks, BLK), NEG_START, jnp.float32),
        jnp.zeros((span_blocks, BLK), jnp.float32),
        jnp.zeros((span_blocks, BLK, head_width), jnp.float32),
    )
    k_blocks = k_head.reshape(span_blocks, BLK, head_width)
    v_blocks = v_head.reshape(span_blocks, BLK, head_width)
    scores = (
        jnp.einsum("pid,pjd->pij", q_blocks, k_blocks, preferred_element_type=jnp.float32) * scaling
    )
    causal = jnp.arange(BLK)[:, None] >= jnp.arange(BLK)[None, :]
    carry_state = absorb(carry_state, scores, causal[None], v_blocks, "pij,pjd->pid")
    ext_k = jnp.concatenate([key_prev, k_head], axis=0)
    ext_v = jnp.concatenate([val_prev, v_head], axis=0)

    def slash_step(turn_index, carry_state):
        offset = s_list[turn_index]
        start_row = span_rows - offset * BLK
        k_tile = lax.dynamic_slice_in_dim(ext_k, start_row, span_rows, 0).reshape(
            span_blocks, BLK, head_width
        )
        v_tile = lax.dynamic_slice_in_dim(ext_v, start_row, span_rows, 0).reshape(
            span_blocks, BLK, head_width
        )
        tile_scores = (
            jnp.einsum("pid,pjd->pij", q_blocks, k_tile, preferred_element_type=jnp.float32)
            * scaling
        )
        key_mask = (block_ids - offset >= 0)[:, None, None]
        return absorb(carry_state, tile_scores, key_mask, v_tile, "pij,pjd->pid")

    carry_state = lax.fori_loop(0, s_count, slash_step, carry_state)

    def vertical_step(turn_index, carry_state):
        column = v_list[turn_index]
        k_tile = sink_k[turn_index]
        v_tile = sink_v[turn_index]
        tile_scores = (
            jnp.einsum("pid,jd->pij", q_blocks, k_tile, preferred_element_type=jnp.float32)
            * scaling
        )
        distance = block_ids - column
        in_slash = (distance <= span_blocks) & slash_table[jnp.clip(distance, 0, span_blocks)]
        key_mask = ((distance > 0) & jnp.logical_not(in_slash))[:, None, None]
        return absorb(carry_state, tile_scores, key_mask, v_tile, "pij,jd->pid")

    carry_state = lax.fori_loop(0, v_count, vertical_step, carry_state)
    run_max, run_sum, run_acc = carry_state
    return (run_acc / run_sum[..., None]).astype(jnp.bfloat16).reshape(span_rows, head_width)


def spans_body(queries, keys, values, vert_idx, vert_cnt, slash_off, slash_cnt):
    n_seq = lax.axis_size("seq")
    heads = queries.shape[2]
    per_dev = heads // n_seq
    head_order = jnp.arange(heads, dtype=jnp.int32)
    q_all, k_all, v_all = (
        lax.all_to_all(queries, "seq", split_axis=2, concat_axis=1, tiled=True),
        lax.all_to_all(keys, "seq", split_axis=2, concat_axis=1, tiled=True),
        lax.all_to_all(values, "seq", split_axis=2, concat_axis=1, tiled=True),
    )
    key_prev, val_prev = from_behind((k_all, v_all), ("qblk", "sub"), 1)
    span_rows = q_all.shape[1]
    head_width = q_all.shape[3]
    span_blocks = span_rows // BLK
    first_block = lax.axis_index(("qblk", "sub")) * span_blocks
    my_heads = lax.dynamic_slice_in_dim(head_order, lax.axis_index("seq") * per_dev, per_dev)
    v_lists = pick_rows(vert_idx, my_heads)
    v_counts = pick_rows(vert_cnt, my_heads)
    s_lists = pick_rows(slash_off, my_heads)
    s_counts = pick_rows(slash_cnt, my_heads)
    local_ids = v_lists - first_block
    owned = (local_ids >= 0) & (local_ids < span_blocks)
    clipped = jnp.clip(local_ids, 0, span_blocks - 1)
    slot_ids = jnp.arange(per_dev, dtype=jnp.int32)[:, None]
    k_grid = k_all[0].reshape(span_blocks, BLK, per_dev, head_width)
    v_grid = v_all[0].reshape(span_blocks, BLK, per_dev, head_width)
    zero_half = jnp.zeros((), jnp.bfloat16)
    picked_k = jnp.where(owned[:, :, None, None], k_grid[clipped, :, slot_ids, :], zero_half)
    picked_v = jnp.where(owned[:, :, None, None], v_grid[clipped, :, slot_ids, :], zero_half)
    sink_k, sink_v = (
        lax.psum(picked_k, ("qblk", "sub")).astype(jnp.float32),
        lax.psum(picked_v, ("qblk", "sub")).astype(jnp.float32),
    )
    sink_k = sink_k.astype(jnp.bfloat16)
    sink_v = sink_v.astype(jnp.bfloat16)
    s_width = slash_off.shape[1]
    s_live = jnp.arange(s_width, dtype=jnp.int32)[None, :] < s_counts[:, None]
    offset_ids = jnp.arange(span_blocks + 1, dtype=jnp.int32)
    slash_tables = jnp.any(
        (s_lists[:, :, None] == offset_ids[None, None, :]) & s_live[:, :, None], axis=1
    )
    results = []
    for slot in range(per_dev):
        results.append(
            attend_head(
                q_all[0, :, slot, :],
                k_all[0, :, slot, :],
                v_all[0, :, slot, :],
                key_prev[0, :, slot, :],
                val_prev[0, :, slot, :],
                sink_k[slot],
                sink_v[slot],
                v_lists[slot],
                v_counts[slot],
                s_lists[slot],
                s_counts[slot],
                slash_tables[slot],
                first_block,
            )
        )
    stacked = jnp.stack(results, axis=1)[None]
    restored = lax.all_to_all(stacked, "seq", split_axis=1, concat_axis=2, tiled=True)
    return restored


GROUP = ("seq", "qblk")
MIB = 2**20
REGROUP_VMEM = 60 * MIB
RUNS = 2
CHUNKS = 4
LOG2_E = 1.4426950408889634
ANY = pl.BlockSpec(memory_space=pl.ANY)
HBM = pl.BlockSpec(memory_space=pltpu.HBM)
SMEM = pl.BlockSpec(memory_space=pltpu.SMEM)
VMEM = pl.BlockSpec(memory_space=pltpu.VMEM)


def swap_with(value, axes, mask):
    count = lax.axis_size(axes)
    return lax.ppermute(value, axes, [(source, source ^ mask) for source in range(count)])


def first_head(place, masks, heads, groups):
    half = groups // 2
    return pl.multiple_of(((place[0] ^ masks[0]) // half) * (heads // 2), heads // 2)


def regroup_kernel(place, *refs, tensors, takes, pieces, groups):
    sources, parts = refs[:tensors], refs[tensors : tensors + len(pieces)]
    staged, turned, load_sem, store_sem = refs[tensors + len(pieces) :]
    count, per_group = turned.shape[0], turned.shape[2]
    tokens, heads = sources[0].shape[:2]
    runs = [pl.ds(run * tokens // RUNS, tokens // RUNS) for run in range(RUNS)]
    loads = []
    for at, (masks, tensor) in enumerate(takes):
        first = first_head(place, masks, heads, groups)
        for into, run in enumerate(runs):
            source = sources[tensor].at[run, pl.ds(first, heads // 2)]
            loads.append(pltpu.make_async_copy(source, staged.at[at, run], load_sem.at[at, into]))
            loads[-1].start()
    stores = []
    for at in range(len(takes)):
        for into, run in enumerate(runs):
            loads[at * RUNS + into].wait()
            heads_first = jnp.swapaxes(staged[at, run], 0, 1)
            for group in range(count):
                turned[group, at, :, run] = heads_first[group * per_group : (group + 1) * per_group]
        for into, ((mask, begin, length), part) in enumerate(zip(pieces, parts)):
            if begin <= at < begin + length:
                source = turned.at[(place[0] ^ mask) % count, at]
                stores.append(
                    pltpu.make_async_copy(source, part.at[at - begin], store_sem.at[into, at - begin])
                )
                stores[-1].start()
    for store in stores:
        store.wait()


def regroup(place, tensors, takes, pieces, groups):
    tokens, heads, width = tensors[0].shape
    part = (heads // groups, tokens, width)
    parts = pl.pallas_call(
        functools.partial(
            regroup_kernel, tensors=len(tensors), takes=takes, pieces=pieces, groups=groups
        ),
        out_shape=[
            jax.ShapeDtypeStruct((length,) + part, jnp.bfloat16) for _, _, length in pieces
        ],
        in_specs=[SMEM] + [HBM] * len(tensors),
        out_specs=[ANY] * len(pieces),
        scratch_shapes=[
            pltpu.VMEM((len(takes), tokens, heads // 2, width), jnp.bfloat16),
            pltpu.VMEM((groups // 2, len(takes)) + part, jnp.bfloat16),
            pltpu.SemaphoreType.DMA((len(takes), RUNS)),
            pltpu.SemaphoreType.DMA((len(pieces), len(takes))),
        ],
        compiler_params=pltpu.CompilerParams(vmem_limit_bytes=REGROUP_VMEM),
        cost_estimate=pl.CostEstimate(flops=1, bytes_accessed=1, transcendentals=0),
        name="regroup",
    )(place, *tensors)
    return dict(zip(pieces, parts))


def ungroup_kernel(place, *refs, masks, groups):
    parts = refs[: len(masks)]
    out, staged, turned, store_sem = refs[-4:]
    count, per_group, _, width = staged.shape
    tokens, heads = out.shape[:2]
    first = first_head(place, masks, heads, groups)
    for part, mask in zip(parts, masks):
        staged[(place[0] ^ mask) % count] = part[...]
    stores = []
    for chunk in range(CHUNKS):
        run = pl.ds(chunk * tokens // CHUNKS, tokens // CHUNKS)
        heads_first = staged[:, :, run].reshape(count * per_group, tokens // CHUNKS, width)
        turned[run] = jnp.swapaxes(heads_first, 0, 1)
        target = out.at[run, pl.ds(first, heads // 2)]
        stores.append(pltpu.make_async_copy(turned.at[run], target, store_sem.at[chunk]))
        stores[-1].start()
    for store in stores:
        store.wait()


def ungroup(place, parts, masks, groups, begun=None):
    per_group, tokens, width = parts[masks[0]].shape
    shape = (tokens, groups * per_group, width)
    return pl.pallas_call(
        functools.partial(ungroup_kernel, masks=masks, groups=groups),
        out_shape=jax.ShapeDtypeStruct(shape, jnp.bfloat16),
        in_specs=[SMEM] + [VMEM] * len(masks) + ([] if begun is None else [HBM]),
        out_specs=HBM,
        scratch_shapes=[
            pltpu.VMEM((len(masks), per_group, tokens, width), jnp.bfloat16),
            pltpu.VMEM((tokens, len(masks) * per_group, width), jnp.bfloat16),
            pltpu.SemaphoreType.DMA((CHUNKS,)),
        ],
        input_output_aliases={} if begun is None else {1 + len(masks): 0},
        compiler_params=pltpu.CompilerParams(vmem_limit_bytes=6 * MIB),
        cost_estimate=pl.CostEstimate(flops=1, bytes_accessed=1, transcendentals=0),
        name="ungroup",
    )(place, *[parts[mask] for mask in masks], *([] if begun is None else [begun]))


def block_of(place, mask, n_seq, n_qblk):
    partner = place[0] ^ mask
    return (2 * (partner % n_qblk) + place[1]) * n_seq + partner // n_qblk


def gather_kernel(place, *refs, groups, n_seq, n_qblk):
    own, out, sem = refs[:groups], refs[groups], refs[groups + 1]
    copies = [
        pltpu.make_async_copy(
            part.at[pl.ds(0, 2)],
            out.at[((place[0] ^ mask) % n_qblk) * n_seq + (place[0] ^ mask) // n_qblk],
            sem.at[mask],
        )
        for mask, part in enumerate(own)
    ]
    for copy in copies:
        copy.start()
    for copy in copies:
        copy.wait()


def gather(place, parts):
    groups = len(parts)
    shape = (groups, 2) + parts[0].shape[1:]
    return pl.pallas_call(
        functools.partial(
            gather_kernel,
            groups=groups,
            n_seq=lax.axis_size("seq"),
            n_qblk=lax.axis_size("qblk"),
        ),
        out_shape=jax.ShapeDtypeStruct(shape, jnp.bfloat16),
        in_specs=[SMEM] + [ANY] * groups,
        out_specs=ANY,
        scratch_shapes=[pltpu.SemaphoreType.DMA((groups,))],
        compiler_params=pltpu.CompilerParams(vmem_limit_bytes=2 * MIB),
        cost_estimate=pl.CostEstimate(flops=1, bytes_accessed=1, transcendentals=0),
        name="gather",
    )(place, *parts)


def attend_kernel(place, tables, *refs, masks, sizes, n_seq, n_qblk, sides):
    count = len(masks)
    loads = []
    if sides:
        sides, queries, outs = refs[:2], refs[2 : 2 + count], refs[2 + count : 2 + 2 * count]
        kv, sem = refs[-2:]
        for at, side in enumerate(sides):
            loads.append(pltpu.make_async_copy(side, kv.at[place[1] ^ at], sem.at[at]))
            loads[-1].start()
    else:
        kv, queries, outs = refs[0], refs[1 : 1 + count], refs[1 + count :]
    heads, width = kv.shape[3], kv.shape[-1]
    scaling = width ** (-0.5) * LOG2_E
    all_heads, n_vert, n_slash = sizes
    vert_cnt = all_heads * n_vert
    slash_off = vert_cnt + all_heads
    slash_cnt = slash_off + all_heads * n_slash
    key_row = lax.broadcasted_iota(jnp.int32, (BLK, BLK), 0)
    query_col = lax.broadcasted_iota(jnp.int32, (BLK, BLK), 1)
    causal = key_row <= query_col

    def tile(block, tensor, slot):
        span = block // n_seq
        return kv[span % 2, (span // 2) * n_seq + block % n_seq, tensor, slot]

    def unit(query, out, slot, block):
        head = place[0] * heads + slot
        vert_live, slash_live = tables[vert_cnt + head], tables[slash_cnt + head]
        offsets = [tables[slash_off + turn * all_heads + head] for turn in range(n_slash)]
        cols, live = [block], []
        for turn, offset in enumerate(offsets):
            live.append((turn < slash_live) & (block >= offset))
            cols.append(jnp.maximum(block - offset, 0))
        for turn in range(n_vert):
            column = tables[turn * all_heads + head]
            distance = block - column
            ok = (turn < vert_live) & (distance > 0)
            for other, offset in enumerate(offsets):
                ok = ok & jnp.logical_not((other < slash_live) & (offset == distance))
            live.append(ok)
            cols.append(column)
        keys = jnp.concatenate([tile(column, 0, slot) for column in cols], axis=0)
        vals = jnp.concatenate([tile(column, 1, slot) for column in cols], axis=0)
        scores = lax.dot_general(
            keys, query[query.shape[0] - 1, slot], (((1,), (1,)), ((), ())), preferred_element_type=jnp.float32
        )
        parts = [jnp.where(causal, scores[:BLK], -jnp.inf)]
        for at, ok in enumerate(live):
            bias = jnp.where(ok, 0.0, -jnp.inf).astype(jnp.float32)
            parts.append(scores[(at + 1) * BLK : (at + 2) * BLK] + bias)
        top = functools.reduce(jnp.maximum, parts)
        top = jnp.max(top, axis=0, keepdims=True)
        weights = [jnp.exp2((part - top) * scaling) for part in parts]
        total = jnp.sum(functools.reduce(jnp.add, weights), axis=0, keepdims=True)
        rounded = jnp.concatenate([weight.astype(jnp.bfloat16) for weight in weights], axis=0)
        acc = lax.dot_general(
            vals, rounded, (((0,), (0,)), ((), ())), preferred_element_type=jnp.float32
        )
        out[slot] = (acc * (1.0 / total)).T.astype(jnp.bfloat16)

    for slot in range(heads):
        for load in loads[2 * slot : 2 * slot + 2]:
            load.wait()
        for mask, query, out in zip(masks, queries, outs):
            unit(query, out, slot, block_of(place, mask, n_seq, n_qblk))


def attend(place, tables, sizes, kv, queries, masks):
    sides, count = isinstance(kv, (tuple, list)), len(masks)
    if sides:
        spots, _, heads, tokens, width = kv[0].shape
        whole = jax.ShapeDtypeStruct((2, spots, 2, heads, tokens, width), jnp.bfloat16)
    else:
        _, _, _, heads, tokens, width = kv.shape
    outs = pl.pallas_call(
        functools.partial(
            attend_kernel,
            masks=masks,
            sizes=sizes,
            n_seq=lax.axis_size("seq"),
            n_qblk=lax.axis_size("qblk"),
            sides=sides,
        ),
        out_shape=[jax.ShapeDtypeStruct((heads, tokens, width), jnp.bfloat16)] * count
        + ([whole] if sides else []),
        in_specs=[SMEM] * 2 + ([ANY] * 2 if sides else [VMEM]) + [VMEM] * count,
        out_specs=[VMEM] * (count + sides),
        scratch_shapes=[pltpu.SemaphoreType.DMA((2,))] if sides else [],
        compiler_params=pltpu.CompilerParams(vmem_limit_bytes=12 * MIB),
        cost_estimate=pl.CostEstimate(flops=1, bytes_accessed=1, transcendentals=0),
        name="attend",
    )(place, tables, *(kv if sides else [kv]), *[queries[mask] for mask in masks])
    return dict(zip(masks, outs)), (outs[-1] if sides else kv)


def after(value, *others):
    return lax.optimization_barrier((value, *others))[0]


def group_body(queries, keys, values, *tables):
    n_seq, n_qblk = lax.axis_size("seq"), lax.axis_size("qblk")
    groups = n_seq * n_qblk
    place = jnp.stack([lax.axis_index(GROUP), lax.axis_index("sub")]).astype(jnp.int32)
    sizes = (queries.shape[2], tables[0].shape[1], tables[2].shape[1])
    flat = jnp.concatenate([table.T.reshape(-1) for table in tables])
    near, far = list(range(groups // 2)), list(range(groups // 2, groups))
    def send(part, mask):
        return swap_with(part, GROUP, mask) if mask else part

    keys, values, queries = keys[0], values[0], queries[0]
    pieces = [(mask, 0, 2) for mask in far]
    kv_far = regroup(place, (keys, values), [(far, 0), (far, 1)], pieces, groups)
    takes = [(near, 0), (near, 1), (near, 2), (far, 2)]
    pieces = [(mask, 0, 3) for mask in near] + [(mask, 3, 1) for mask in far]
    rest = regroup(place, (keys, values, after(queries, flat)), takes, pieces, groups)
    got = {mask: send(rest[mask, 0, 3], mask) for mask in near}
    got.update({mask: send(kv_far[mask, 0, 2], mask) for mask in far})

    def share(*parts):
        own = gather(place, parts)
        return own, swap_with(own, "sub", 1)

    def share_again(*parts):
        own = gather(place, parts)
        return own, swap_with(after(own, place), "sub", 1)

    some = tables[1][0] >= 1
    sides = lax.cond(some, share, share_again, *[got[mask] for mask in range(groups)])
    arrived = {mask: got[mask] for mask in near}
    arrived.update({mask: send(rest[mask, 3, 1], mask) for mask in far})
    cut = len(far) // 2
    outs, kv = attend(place, flat, sizes, sides, arrived, near + far[:cut])
    outs.update(attend(place, flat, sizes, kv, arrived, far[cut:])[0])
    back = {mask: send(outs[mask], mask) for mask in near}
    back.update({mask: send(outs[mask], mask) for mask in far})
    begun = ungroup(place, back, near, groups)
    return ungroup(place, back, far, groups, begun)[None]


def body(queries, keys, values, *tables):
    groups, heads = lax.axis_size(GROUP), queries.shape[2]
    fits = heads % groups == 0 and heads % 32 == 0 and queries.shape[:2] == (1, BLK)
    if fits and groups & (groups - 1) == 0 and lax.axis_size("sub") == 2:
        return group_body(queries, keys, values, *tables)
    return spans_body(queries, keys, values, *tables)


def solution(mesh):
    placed = (
        P(("groups", "qblk", "sub"), "seq", None, None),
        P(("groups", "qblk", "sub"), "seq", None, None),
        P(("groups", "qblk", "sub"), "seq", None, None),
        P("groups", None),
        P("groups"),
        P("groups", None),
        P("groups"),
    )
    return jax.shard_map(
        body,
        mesh=mesh,
        in_specs=placed,
        out_specs=P(("groups", "qblk", "sub"), "seq", None, None),
        check_vma=False,
    )
```
